256 devices in a mesh: dp: 4 (over x_hi, core), in: 4 (over y), out: 16 (over z, x_lo).
Axes of the slice: x: 4 (x_hi: 2, x_lo: 2; x = x_hi * 2 + x_lo), y: 4, z: 8, core: 2. Of those that a mesh axis runs over, the one named last changes fastest.
Arguments:
- inputs: bfloat16 [512, 8192], P(('dp', 'out'), 'in'), may hold values from -6 to 6
- context: bfloat16 [512, 4096], P('dp', 'out'), may hold values from -6 to 6
- gate_blocks: bfloat16 [4, 16, 240, 4096], P('in', 'out'), may hold values from -0.09375 to 0.09375
- gate_ids: int32 [4, 16, 240], P('in', 'out'), may hold values from 0 to 447, as said below
- gate_count: int32 [4, 16], P('in', 'out'), may hold values from 180 to 240
- up_blocks: bfloat16 [4, 16, 240, 4096], P('in', 'out'), may hold values from -0.09375 to 0.09375
- up_ids: int32 [4, 16, 240], P('in', 'out'), may hold values from 0 to 447, as said below
- up_count: int32 [4, 16], P('in', 'out'), may hold values from 180 to 240
- down_blocks: bfloat16 [16, 4, 240, 4096], P('out', 'in'), may hold values from -0.0625 to 0.0625
- down_ids: int32 [16, 4, 240], P('out', 'in'), may hold values from 0 to 447, as said below
- down_count: int32 [16, 4], P('out', 'in'), may hold values from 180 to 240
- heads_blocks: bfloat16 [16, 4, 68, 4096], P('out', 'in'), may hold values from -0.125 to 0.125
- heads_ids: int32 [16, 4, 68], P('out', 'in'), may hold values from 0 to 127, as said below
- heads_count: int32 [16, 4], P('out', 'in'), may hold values from 51 to 68
- cotangent: bfloat16 [512, 8192], P(('dp', 'out'), 'in'), may hold values from -6 to 6
Outputs:
- layer_output: bfloat16 [512, 8192], P(('dp', 'out'), 'in')
- input_grad: bfloat16 [512, 8192], P(('dp', 'out'), 'in')
- context_grad: bfloat16 [512, 4096], P('dp', 'out')
- gate_grads: bfloat16 [4, 16, 240, 4096], P('in', 'out', 'dp')
- up_grads: bfloat16 [4, 16, 240, 4096], P('in', 'out', 'dp')
- down_grads: bfloat16 [16, 4, 240, 4096], P('out', 'in', 'dp')
- heads_grads: bfloat16 [16, 4, 68, 4096], P('out', 'in', 'dp')
The draws below stay inside these ranges and needn't reach their ends.
Inputs may be any that keep to these rules, and one draw needn't show every extreme that they name: `gate_ids`: entry r * 14 + c names block row r and block column c of a gate shard; all entries of one shard's list are distinct. `up_ids`: entry r * 14 + c names block row r and block column c of an up shard; all entries of one shard's list are distinct. `down_ids`: entry r * 32 + c names block row r (hidden units) and block column c (model width) of a down shard; all entries of one shard's list are distinct. `heads_ids`: entry r * 32 + c names block row r (attention features) and block column c (model width) of a shard; all entries of one shard's list are distinct.
All inputs are finite; a program needn't handle non-finite values.
Results may differ from the reference program's by a relative error of at most 0.039.
Values may be sent and summed in bfloat16 or wider, within the bound.
A program may use at most 128 MiB of HBM per device.

```python
import jax
import jax.numpy as jnp
from jax import lax

D = 8192
FF = 14336
CTX = 4096
BLOCK = 64
TOKENS = 512
DB = 32
FB = 14
CB = 4
NBG = 240
NBO = 68
N_DP = 4
N_IN = 4
N_OUT = 16


def shard_lists(key, lead_a, lead_b, pool, keep):
    keys_all = jax.random.split(key, lead_a * lead_b)
    chosen = jax.vmap(lambda single: jax.random.permutation(single, pool)[:keep])(keys_all)
    return chosen.reshape(lead_a, lead_b, keep).astype(jnp.int32)


def shard_counts(key, lead_a, lead_b, keep):
    first_key, second_key = jax.random.split(key)
    counts = jax.random.randint(first_key, (lead_a * lead_b,), keep - keep // 4, keep + 1, dtype=jnp.int32)
    fullest = jax.random.randint(second_key, (), 0, lead_a * lead_b, dtype=jnp.int32)
    counts = counts.at[fullest].set(keep)
    return counts.reshape(lead_a, lead_b)


def draw_gate_ids(key, part):
    return shard_lists(jax.random.fold_in(key, 101), N_IN, N_OUT, DB * FB, NBG)


def draw_up_ids(key, part):
    return shard_lists(jax.random.fold_in(key, 202), N_IN, N_OUT, DB * FB, NBG)


def draw_down_ids(key, part):
    return shard_lists(jax.random.fold_in(key, 303), N_OUT, N_IN, DB * FB, NBG)


def draw_heads_ids(key, part):
    return shard_lists(jax.random.fold_in(key, 404), N_OUT, N_IN, CB * DB, NBO)


def draw_gate_count(key, part):
    return shard_counts(jax.random.fold_in(key, 111), N_IN, N_OUT, NBG)


def draw_up_count(key, part):
    return shard_counts(jax.random.fold_in(key, 222), N_IN, N_OUT, NBG)


def draw_down_count(key, part):
    return shard_counts(jax.random.fold_in(key, 333), N_OUT, N_IN, NBG)


def draw_heads_count(key, part):
    return shard_counts(jax.random.fold_in(key, 444), N_OUT, N_IN, NBO)


def level_of(stream_key, shape, shards, low, high):
    gain = 1.0
    for dim, parts in shards:
        draws = jax.random.uniform(jax.random.fold_in(jax.random.fold_in(stream_key, 6), dim), (parts,), jnp.float32, low / len(shards), high / len(shards))
        gain = gain * jnp.repeat(jnp.exp(draws), shape[dim] // parts).reshape((-1,) + (1,) * (len(shape) - 1 - dim))
    return gain


def bell_draw(stream_key, extent, spread, most, shards=(), kind=jnp.bfloat16):
    result = spread * jax.random.normal(stream_key, extent, jnp.float32)
    if shards:
        result = result * level_of(stream_key, extent, shards, -0.22, 0.18)
    return jnp.clip(result, -most, most).astype(kind)


def setup_inputs(seed: int = 0) -> dict:
    arg_keys = jax.random.split(jax.random.key(seed), 16)
    inputs = bell_draw(arg_keys[0], (TOKENS, D), 1.0, 6.0, ((0, 64), (1, 4)))
    context = bell_draw(arg_keys[1], (TOKENS, CTX), 1.0, 6.0, ((0, 4), (1, 16)))
    gate_blocks = bell_draw(arg_keys[2], (N_IN, N_OUT, NBG, BLOCK * BLOCK), (D // 2) ** -0.5, 0.09375, ((0, 4), (1, 16)))
    gate_ids = draw_gate_ids(jax.random.fold_in(arg_keys[15], 71), 0)
    gate_count = draw_gate_count(jax.random.fold_in(arg_keys[15], 71), 0)
    up_blocks = bell_draw(arg_keys[5], (N_IN, N_OUT, NBG, BLOCK * BLOCK), (D // 2) ** -0.5, 0.09375, ((0, 4), (1, 16)))
    up_ids = draw_up_ids(jax.random.fold_in(arg_keys[15], 71), 0)
    up_count = draw_up_count(jax.random.fold_in(arg_keys[15], 71), 0)
    down_blocks = bell_draw(arg_keys[8], (N_OUT, N_IN, NBG, BLOCK * BLOCK), (FF // 2) ** -0.5, 0.0625, ((0, 16), (1, 4)))
    down_ids = draw_down_ids(jax.random.fold_in(arg_keys[15], 71), 0)
    down_count = draw_down_count(jax.random.fold_in(arg_keys[15], 71), 0)
    heads_blocks = bell_draw(arg_keys[11], (N_OUT, N_IN, NBO, BLOCK * BLOCK), (CTX // 2) ** -0.5, 0.125, ((0, 16), (1, 4)))
    heads_ids = draw_heads_ids(jax.random.fold_in(arg_keys[15], 71), 0)
    heads_count = draw_heads_count(jax.random.fold_in(arg_keys[15], 71), 0)
    cotangent = bell_draw(arg_keys[14], (TOKENS, D), 1.0, 6.0, ((0, 64), (1, 4)))
    return {"inputs": inputs, "context": context, "gate_blocks": gate_blocks, "gate_ids": gate_ids, "gate_count": gate_count, "up_blocks": up_blocks, "up_ids": up_ids, "up_count": up_count, "down_blocks": down_blocks, "down_ids": down_ids, "down_count": down_count, "heads_blocks": heads_blocks, "heads_ids": heads_ids, "heads_count": heads_count, "cotangent": cotangent}


def shard_index(slot_ids):
    lead_a, lead_b, slot_total = slot_ids.shape
    index_a = jnp.arange(lead_a, dtype=jnp.int32)[:, None, None]
    index_b = jnp.arange(lead_b, dtype=jnp.int32)[None, :, None]
    return (index_a, index_b)

def present_mask(slot_ids, counts):
    slot_total = slot_ids.shape[-1]
    return jnp.arange(slot_total, dtype=jnp.int32)[None, None, :] < counts[:, :, None]

def place_blocks(blocks, slot_ids, counts, block_rows, block_cols):
    lead_a, lead_b, slot_total = slot_ids.shape
    present = present_mask(slot_ids, counts)
    pieces = blocks.reshape(lead_a, lead_b, slot_total, BLOCK, BLOCK)
    pieces = jnp.where(present[..., None, None], pieces, jnp.zeros_like(pieces))
    index_a, index_b = shard_index(slot_ids)
    row_ids = (slot_ids // block_cols).astype(jnp.int32)
    col_ids = (slot_ids % block_cols).astype(jnp.int32)
    filled = jnp.zeros((lead_a, block_rows, BLOCK, lead_b, block_cols, BLOCK), blocks.dtype)
    filled = filled.at[index_a, row_ids, :, index_b, col_ids, :].add(pieces)
    return filled.reshape(lead_a * block_rows * BLOCK, lead_b * block_cols * BLOCK)

def pick_blocks(matrix, slot_ids, counts, block_rows, block_cols):
    lead_a, lead_b, slot_total = slot_ids.shape
    present = present_mask(slot_ids, counts)
    index_a, index_b = shard_index(slot_ids)
    shaped = matrix.reshape(lead_a, block_rows, BLOCK, lead_b, block_cols, BLOCK)
    pieces = shaped[index_a, (slot_ids // block_cols).astype(jnp.int32), :, index_b, (slot_ids % block_cols).astype(jnp.int32), :]
    pieces = pieces.reshape(lead_a, lead_b, slot_total, BLOCK * BLOCK)
    return jnp.where(present[..., None], pieces, jnp.zeros_like(pieces))

def block_grad(left_side, right_side, slot_ids, counts, block_rows, block_cols):
    group_rows = left_side.shape[0] // N_DP
    running = None
    for group_index in range(N_DP):
        left_part = left_side[group_index * group_rows:(group_index + 1) * group_rows]
        right_part = right_side[group_index * group_rows:(group_index + 1) * group_rows]
        product = jnp.dot(left_part.T, right_part, preferred_element_type=jnp.float32)
        picked = pick_blocks(product, slot_ids, counts, block_rows, block_cols)
        rounded = lax.optimization_barrier(picked.astype(jnp.bfloat16))
        widened = rounded.astype(jnp.float32)
        running = widened if running is None else running + widened
    return running.astype(jnp.bfloat16)

def reference(inputs, context, gate_blocks, gate_ids, gate_count, up_blocks, up_ids, up_count, down_blocks, down_ids, down_count, heads_blocks, heads_ids, heads_count, cotangent):
    gate_matrix = place_blocks(gate_blocks, gate_ids, gate_count, DB, FB)
    up_matrix = place_blocks(up_blocks, up_ids, up_count, DB, FB)
    down_matrix = place_blocks(down_blocks, down_ids, down_count, FB, DB)
    heads_matrix = place_blocks(heads_blocks, heads_ids, heads_count, CB, DB)
    attention = jnp.dot(context, heads_matrix, preferred_element_type=jnp.float32)
    residual = (inputs.astype(jnp.float32) + attention).astype(jnp.bfloat16)
    gate_sum = jnp.dot(residual, gate_matrix, preferred_element_type=jnp.float32)
    up_sum = jnp.dot(residual, up_matrix, preferred_element_type=jnp.float32)
    sigmoid_gate = jax.nn.sigmoid(gate_sum)
    hidden = (gate_sum * sigmoid_gate * up_sum).astype(jnp.bfloat16)
    mlp_term = jnp.dot(hidden, down_matrix, preferred_element_type=jnp.float32)
    layer_output = (residual.astype(jnp.float32) + mlp_term).astype(jnp.bfloat16)
    hidden_grad = jnp.dot(cotangent, down_matrix.T, preferred_element_type=jnp.float32)
    gate_delta = (hidden_grad * up_sum * sigmoid_gate * (1.0 + gate_sum * (1.0 - sigmoid_gate))).astype(jnp.bfloat16)
    up_delta = (hidden_grad * gate_sum * sigmoid_gate).astype(jnp.bfloat16)
    back_term = jnp.dot(gate_delta, gate_matrix.T, preferred_element_type=jnp.float32) + jnp.dot(up_delta, up_matrix.T, preferred_element_type=jnp.float32)
    input_grad = (cotangent.astype(jnp.float32) + back_term).astype(jnp.bfloat16)
    context_grad = jnp.dot(input_grad, heads_matrix.T, preferred_element_type=jnp.float32).astype(jnp.bfloat16)
    gate_grads = block_grad(residual, gate_delta, gate_ids, gate_count, DB, FB)
    up_grads = block_grad(residual, up_delta, up_ids, up_count, DB, FB)
    down_grads = block_grad(hidden, cotangent, down_ids, down_count, FB, DB)
    heads_grads = block_grad(context, input_grad, heads_ids, heads_count, CB, DB)
    return (layer_output, input_grad, context_grad, gate_grads, up_grads, down_grads, heads_grads)
```

```python
import jax
import jax.numpy as jnp
from jax import lax
from jax.experimental import pallas as pl
from jax.experimental.pallas import tpu as pltpu
from jax.sharding import PartitionSpec as P

BLOCK = 64
CELL = BLOCK * BLOCK
BF = jnp.bfloat16
F32 = jnp.float32
MESH = pl.DeviceIdType.MESH
VM = pl.BlockSpec(memory_space=pltpu.VMEM)
ANY = pl.BlockSpec(memory_space=pl.ANY)


def dot(a, b):
    return lax.dot_general(a, b, (((1,), (0,)), ((), ())), preferred_element_type=F32)


def dot_nt(a, b):
    return lax.dot_general(a, b, (((1,), (1,)), ((), ())), preferred_element_type=F32)


def dot_tn(a, b):
    return lax.dot_general(a, b, (((0,), (0,)), ((), ())), preferred_element_type=F32)


def one_hot(row, positions):
    spots = lax.broadcasted_iota(jnp.int32, (positions, row.shape[1]), 0)
    return jnp.where(spots == row, 1.0, 0.0).astype(BF)


def swap_matrix(inner, outer):
    rows = lax.broadcasted_iota(jnp.int32, (inner * outer, inner * outer), 0)
    cols = lax.broadcasted_iota(jnp.int32, (inner * outer, inner * outer), 1)
    source = (rows % outer) * inner + rows // outer
    return jnp.where(cols == source, 1.0, 0.0).astype(BF)


def halves(first, second):
    low = lax.broadcasted_iota(jnp.int32, first.shape, 1) < BLOCK
    return (
        jnp.where(low, first, pltpu.roll(second, BLOCK, 1)),
        jnp.where(low, pltpu.roll(first, BLOCK, 1), second),
    )


def place(hot, swap, blocks, stage, out, inner, used, row0):
    chunk = 256 // inner
    width = out.shape[1]

    def step(k, _):
        lanes = pl.ds(pl.multiple_of(k * chunk * BLOCK, chunk * BLOCK), chunk * BLOCK)
        flat = dot(hot, blocks[:, lanes])
        for p in range(chunk // 2):
            for q in range(width // 128):
                left = flat[2 * q * inner:(2 * q + 1) * inner, p * 128:(p + 1) * 128]
                right = flat[(2 * q + 1) * inner:(2 * q + 2) * inner, p * 128:(p + 1) * 128]
                pair = jnp.concatenate(halves(left, right), axis=0).astype(BF)
                stage[2 * p * inner:(2 * p + 2) * inner, q * 128:(q + 1) * 128] = pair
        dense = dot(swap, stage[:, :width]).astype(BF)
        for r in range(used):
            at = pl.multiple_of(row0 + r * BLOCK + k * chunk, 16)
            out[pl.ds(at, chunk), :] = dense[r * chunk:(r + 1) * chunk]
        return 0

    lax.fori_loop(0, BLOCK // chunk, step, 0)


def place_kernel(idx, gate, up, down, heads, context, wg, wu, wd, wh, term, stage):
    swap8 = swap_matrix(8, 32)
    swap16 = swap_matrix(16, 16)
    place(one_hot(idx[3:4, :heads.shape[0]], 256), swap8, heads, stage, wh, 8, 4, 0)
    for t in range(4):
        cols = slice(t * 512, (t + 1) * 512)
        term[:, cols] = dot(context[...], wh[:, cols]).astype(BF)
    slots = gate.shape[0]
    for row, blocks, out in ((0, gate, wg), (1, up, wu)):
        hot = one_hot(idx[row:row + 1, :slots], 448)
        for s in range(2):
            place(hot[s * 224:(s + 1) * 224], swap16, blocks, stage, out, 16, 16, s * 1024)
    place(one_hot(idx[2:3, :slots], 512), swap16, down, stage, wd, 16, 14, 0)


def place_call(idx, gate, up, down, heads, context):
    shapes = [
        jax.ShapeDtypeStruct((2048, 896), BF),
        jax.ShapeDtypeStruct((2048, 896), BF),
        jax.ShapeDtypeStruct((896, 2048), BF),
        jax.ShapeDtypeStruct((256, 2048), BF),
        jax.ShapeDtypeStruct((128, 2048), BF),
    ]
    return pl.pallas_call(
        place_kernel,
        out_shape=shapes,
        in_specs=[VM] * 6,
        out_specs=[VM] * 5,
        scratch_shapes=[pltpu.VMEM((256, 2048), BF)],
        compiler_params=pltpu.CompilerParams(vmem_limit_bytes=56 * 2**20),
        name="place",
    )(idx, gate, up, down, heads, context)


def pick(left, rights, hots, outs, flats, swap, turned, inner, used, stripes):
    chunk = 256 // inner
    span = used * BLOCK
    for s in range(stripes * span // 128):
        turned[s * 128:(s + 1) * 128, :] = left[:, s * 128:(s + 1) * 128].T

    def step(k, _):
        lanes = pl.ds(pl.multiple_of(k * chunk * BLOCK, chunk * BLOCK), chunk * BLOCK)
        for s in range(stripes):
            rows = [
                turned[pl.ds(pl.multiple_of(s * span + r * BLOCK + k * chunk, 16), chunk), :]
                for r in range(used)
            ]
            rows += [jnp.zeros_like(rows[0])] * (inner - used)
            ordered = dot(swap, jnp.concatenate(rows, axis=0)).astype(BF)
            for right, flat in zip(rights, flats):
                width = right.shape[1]
                base = s * (width // BLOCK) * inner
                piece = 512 if width % 512 == 0 else 896
                for t in range(width // piece):
                    grad = dot(ordered, right[:, t * piece:(t + 1) * piece])
                    for q in range(piece // 128):
                        for p in range(chunk // 2):
                            pair = grad[2 * p * inner:(2 * p + 2) * inner, q * 128:(q + 1) * 128]
                            both = jnp.concatenate(halves(pair[:inner], pair[inner:]), axis=0)
                            at = base + (t * piece // 128 + q) * 2 * inner
                            flat[at:at + 2 * inner, p * 128:(p + 1) * 128] = both.astype(BF)
        for hot, flat, out in zip(hots, flats, outs):
            depth = hot.shape[0]
            picked = dot_tn(hot, flat[:depth, :chunk * BLOCK])
            out[:, lanes] = picked[:out.shape[0]].astype(BF)
        return 0

    lax.fori_loop(0, BLOCK // chunk, step, 0)


def grads_kernel(idx, res, cot, ig, hid, gd, ud, ctx, og, ou, od, oh, turned, flat_a, flat_b):
    swap16 = swap_matrix(16, 16)

    def hot(row, positions):
        return one_hot(idx[row:row + 1, :128], positions)

    pick(res, (gd, ud), (hot(4, 448), hot(5, 448)), (og, ou), (flat_a, flat_b), swap16, turned, 16, 16, 2)
    pick(hid, (cot,), (hot(6, 512),), (od,), (flat_a,), swap16, turned, 16, 14, 1)
    pick(ctx, (ig,), (hot(7, 256),), (oh,), (flat_a,), swap_matrix(32, 8), turned, 8, 4, 1)


def grads_call(idx, res, cot, ig, hid, gd, ud, ctx):
    shapes = [jax.ShapeDtypeStruct((n, CELL), BF) for n in (60, 60, 60, 17)]
    return pl.pallas_call(
        grads_kernel,
        out_shape=shapes,
        in_specs=[VM] * 8,
        out_specs=[VM] * 4,
        scratch_shapes=[
            pltpu.VMEM((2048, 512), BF),
            pltpu.VMEM((512, 2048), BF),
            pltpu.VMEM((512, 2048), BF),
        ],
        compiler_params=pltpu.CompilerParams(vmem_limit_bytes=56 * 2**20),
        name="grads",
    )(idx, res, cot, ig, hid, gd, ud, ctx)


class Links:

    def __init__(self):
        self.dp, self.y, self.out = lax.axis_index("dp"), lax.axis_index("in"), lax.axis_index("out")
        self.depth = lax.axis_size("out") // 2
        self.tall = lax.axis_size("in")
        self.core, self.z = self.dp % 2, self.out // 2
        self.low = self.out % 2
        self.x = (self.dp // 2) * 2 + self.low

    def at_x(self, k):
        x = (self.x + k) % 4
        return (x // 2) * 2 + self.core, self.y, self.z * 2 + x % 2

    def at_z(self, k):
        return self.dp, self.y, ((self.z + k) % self.depth) * 2 + self.low

    def at_y(self, k):
        return self.dp, (self.y + k) % self.tall, self.out

    def sibling(self):
        return (self.dp // 2) * 2 + 1 - self.core, self.y, self.out

    def beside(self):
        return self.dp, self.y, self.z * 2 + 1 - self.low

    def across(self):
        return (self.dp + 2) % 4, self.y, self.out

    def greet(self):
        barrier = pltpu.get_barrier_semaphore()
        peers = [self.at_x(k) for k in (1, 2, 3)]
        peers += [self.at_z(k) for k in range(1, self.depth)]
        peers += [self.at_y(k) for k in range(1, self.tall)]
        peers += [self.sibling()]
        for peer in peers:
            pl.semaphore_signal(barrier, inc=1, device_id=peer, device_id_type=MESH)
        pl.semaphore_wait(barrier, len(peers))


def send(source, target, sems, k, to):
    copy = pltpu.make_async_remote_copy(
        src_ref=source,
        dst_ref=target,
        send_sem=sems.at[0, k],
        recv_sem=sems.at[1, k],
        device_id=to,
        device_id_type=MESH,
    )
    copy.start()
    return copy


class Spread:

    def __init__(self, me, whole, sems):
        self.me, self.whole, self.sems = me, whole, sems
        self.low = pl.ds(pl.multiple_of(me.low * 1024, 1024), 1024)

    def rows(self, dp):
        return pl.ds(pl.multiple_of(dp * 128, 128), 128)

    def over_z(self, own):
        me = self.me
        spot = self.whole.at[pl.ds(pl.multiple_of(me.dp * 128 + me.z * 16, 16), 16), self.low]
        spot[...] = own
        self.first = [send(spot, spot, self.sems, k - 1, me.at_z(k)) for k in range(1, me.depth)]

    def over_x(self):
        me = self.me
        for copy in self.first:
            copy.wait_recv()
        strip = self.whole.at[self.rows(me.dp), self.low]
        near = jnp.where(me.low == 0, 1, 3)
        self.near = send(strip, strip, self.sems, 7, me.beside())
        self.wide = [
            send(strip, strip, self.sems, 8, me.at_x(4 - near)),
            send(strip, strip, self.sems, 9, me.at_x(2)),
        ]

    def group(self):
        self.near.wait_recv()
        return self.rows(self.me.dp)

    def over_cores(self):
        me = self.me
        for copy in self.wide:
            copy.wait_recv()
        self.cores = []
        for k, dp in enumerate((me.dp, (me.dp + 2) % 4)):
            part = self.whole.at[self.rows(dp), :]
            self.cores.append(send(part, part, self.sems, 10 + k, me.sibling()))

    def finish(self):
        for copy in self.cores:
            copy.wait_recv()
        for copy in self.first + [self.near] + self.wide + self.cores:
            copy.wait_send()


class Collect:

    def __init__(self, me, term, half, sums, parts, sems):
        self.me, self.term, self.half, self.sums, self.parts, self.sems = me, term, half, sums, parts, sems

    def over_x(self):
        away = pl.ds(pl.multiple_of((1 - self.me.low) * 1024, 1024), 1024)
        self.near = send(self.term.at[:, away], self.half, self.sems, 7, self.me.beside())

    def over_z(self):
        me = self.me
        self.near.wait_recv()
        home = pl.ds(pl.multiple_of(me.low * 1024, 1024), 1024)
        self.sums[...] = (self.term[:, home].astype(F32) + self.half[...].astype(F32)).astype(BF)
        self.far = []
        for k in range(1, me.depth):
            z = (me.z + k) % me.depth
            chunk = self.sums.at[pl.ds(pl.multiple_of(z * 16, 16), 16), :]
            self.far.append(send(chunk, self.parts.at[k - 1], self.sems, k - 1, me.at_z(k)))

    def total(self):
        me = self.me
        rows = pl.ds(pl.multiple_of(me.z * 16, 16), 16)
        total = self.sums[rows, :].astype(F32)
        for k in range(1, me.depth):
            self.far[k - 1].wait_recv()
            total = total + self.parts[k - 1].astype(F32)
        return total

    def finish(self):
        self.near.wait_send()
        for copy in self.far:
            copy.wait_send()


def swap_out(me, total, outgoing, landing, sems, k):
    outgoing[...] = total
    away = outgoing.at[pl.ds(pl.multiple_of((1 - me.low) * 8, 8), 8), :]
    lanes = pl.ds(pl.multiple_of(me.low * 1024, 1024), 1024)
    landing[:, lanes] = outgoing[pl.ds(pl.multiple_of(me.low * 8, 8), 8), :]
    return send(away, landing.at[:, lanes], sems, k, me.beside())


def chain_kernel(
    x8, cot8, context, term, wg, wu, wd, wh,
    layer, input_grad, context_grad, res, cot, ig, mid, ctx,
    cells, edge, halves_in, sums, parts, backs,
    shares, shares_bf, gathered, swap_from, swap_to, near_sums,
    sem_res, sem_cot, sem_ig, sem_rs, sem_ctx, sem_sum, sem_mid, sem_cg, sem_swap,
):
    me = Links()
    me.greet()
    low8 = pl.ds(pl.multiple_of(me.low * 8, 8), 8)
    away = pl.ds(pl.multiple_of((1 - me.low) * 1024, 1024), 1024)
    home = pl.ds(pl.multiple_of(me.low * 1024, 1024), 1024)

    cells[0] = x8[...].astype(F32)
    cells[1] = cot8[...].astype(F32)
    edge[:, low8, :] = cells[:, :, home]
    entry = send(cells.at[:, :, away], edge.at[:, low8, :], sem_swap, 0, me.beside())
    attention = Collect(me, term, halves_in.at[0], sums.at[0], parts.at[0], sem_rs.at[0])
    attention.over_x()

    own_ctx = pl.ds(pl.multiple_of(me.dp * 128, 128), 128)
    ctx[own_ctx, :] = context[...]
    spot = ctx.at[own_ctx, :]
    ctx_copies = [send(spot, spot, sem_ctx, k, to) for k, to in enumerate((me.sibling(), me.across()))]

    entry.wait_recv()
    spread_cot = Spread(me, cot, sem_cot)
    spread_cot.over_z(edge[1].astype(BF))
    attention.over_z()
    spread_cot.over_x()

    residual = edge[0] + attention.total()
    spread_res = Spread(me, res, sem_res)
    spread_res.over_z(residual.astype(BF))

    def share(slot):
        copies = []
        for k in range(1, me.tall):
            rows = pl.ds(pl.multiple_of(((me.y + k) % me.tall) * 32, 32), 32)
            copies.append(
                send(shares_bf.at[slot, rows, :], gathered.at[k - 1, slot], sem_sum.at[slot], k - 1, me.at_y(k))
            )
        return copies

    rows = spread_cot.group()

    def grad_hidden(t, _):
        lanes = pl.ds(pl.multiple_of(t * 128, 128), 128)
        shares[2, :, lanes] = dot_nt(cot[rows, :], wd[lanes, :])
        return 0

    lax.fori_loop(0, 7, grad_hidden, 0)
    shares_bf[2] = shares[2].astype(BF)
    spread_res.over_x()
    sum_copies = {2: share(2)}

    rows = spread_res.group()
    for slot, weight in ((0, wg), (1, wu)):

        def fan(t, _, weight=weight, slot=slot):
            lanes = pl.ds(pl.multiple_of(t * 128, 128), 128)
            shares[slot, :, lanes] = dot(res[rows, :], weight[:, lanes])
            return 0

        lax.fori_loop(0, 7, fan, 0)
        shares_bf[slot] = shares[slot].astype(BF)
        sum_copies[slot] = share(slot)

    spread_cot.over_cores()
    quarter = pl.ds(pl.multiple_of(me.y * 32, 32), 32)
    totals = []
    for slot in (2, 0, 1):
        total = shares[slot, quarter, :]
        for k in range(me.tall - 1):
            sum_copies[slot][k].wait_recv()
            total = total + gathered[k, slot].astype(F32)
        totals.append(total)
    hidden_grad, gate_sum, up_sum = totals
    sigmoid = 1.0 / (1.0 + jnp.exp(-gate_sum))
    spot_rows = pl.ds(pl.multiple_of(me.dp * 128 + me.y * 32, 32), 32)
    mid[0, spot_rows, :] = (gate_sum * sigmoid * up_sum).astype(BF)
    mid[1, spot_rows, :] = (
        hidden_grad * up_sum * sigmoid * (1.0 + gate_sum * (1.0 - sigmoid))
    ).astype(BF)
    mid[2, spot_rows, :] = (hidden_grad * gate_sum * sigmoid).astype(BF)
    spot = mid.at[:, spot_rows, :]
    mid_copies = [send(spot, spot, sem_mid, k - 1, me.at_y(k)) for k in range(1, me.tall)]
    mid_across = send(spot, spot, sem_mid, 3, me.across())
    spread_res.over_cores()
    for copy in mid_copies:
        copy.wait_recv()

    rows = pl.ds(pl.multiple_of(me.dp * 128, 128), 128)

    def back(t, _):
        lanes = pl.ds(pl.multiple_of(t * 256, 256), 256)
        backs[0, :, lanes] = (
            dot_nt(mid[1, rows, :], wg[lanes, :]) + dot_nt(mid[2, rows, :], wu[lanes, :])
        ).astype(BF)
        return 0

    lax.fori_loop(0, 8, back, 0)
    backward = Collect(me, backs.at[0], halves_in.at[1], sums.at[1], parts.at[1], sem_rs.at[1])
    backward.over_x()

    def forth(t, _):
        lanes = pl.ds(pl.multiple_of(t * 256, 256), 256)
        backs[1, :, lanes] = dot(mid[0, rows, :], wd[:, lanes]).astype(BF)
        return 0

    lax.fori_loop(0, 8, forth, 0)
    forward = Collect(me, backs.at[1], halves_in.at[2], sums.at[2], parts.at[2], sem_rs.at[2])
    forward.over_x()
    backward.over_z()
    forward.over_z()

    mid_across.wait_recv()
    spot = mid.at[:, pl.ds(pl.multiple_of(((me.dp + 2) % 4) * 128 + me.y * 32, 32), 32), :]
    mid_far = [send(spot, spot, sem_mid, 3 + k, me.at_y(k)) for k in range(1, me.tall)]

    total = edge[1] + backward.total()
    spread_ig = Spread(me, ig, sem_ig)
    spread_ig.over_z(total.astype(BF))
    swap_ig = swap_out(me, total, swap_from.at[0], swap_to.at[0], sem_swap, 1)
    total = residual.astype(BF).astype(F32) + forward.total()
    swap_layer = swap_out(me, total, swap_from.at[1], swap_to.at[1], sem_swap, 2)

    for copy in mid_far:
        copy.wait_recv()
    mid_cores = []
    for k, dp in enumerate((me.dp, (me.dp + 2) % 4)):
        spot = mid.at[:, pl.ds(pl.multiple_of(dp * 128, 128), 128), :]
        mid_cores.append(send(spot, spot, sem_mid, 7 + k, me.sibling()))

    spread_ig.over_x()
    rows = spread_ig.group()
    near_sums[me.y] = dot_nt(ig[rows, :], wh[...]).astype(BF)
    spot = near_sums.at[me.y]
    cg_copies = [send(spot, spot, sem_cg, k - 1, me.at_y(k)) for k in range(1, me.tall)]

    ctx_copies[1].wait_recv()
    spot = ctx.at[pl.ds(pl.multiple_of(((me.dp + 2) % 4) * 128, 128), 128), :]
    ctx_copies.append(send(spot, spot, sem_ctx, 2, me.sibling()))
    swap_ig.wait_recv()
    input_grad[...] = swap_to[0].astype(BF)
    swap_layer.wait_recv()
    layer[...] = swap_to[1].astype(BF)
    spread_ig.over_cores()

    for copy in cg_copies:
        copy.wait_recv()
    total = near_sums[0].astype(F32)
    for k in range(1, me.tall):
        total = total + near_sums[k].astype(F32)
    context_grad[...] = total.astype(BF)

    for spread in (spread_cot, spread_res, spread_ig):
        spread.finish()
    for collect in (attention, backward, forward):
        collect.finish()
    for copy in mid_cores + [ctx_copies[0], ctx_copies[2]]:
        copy.wait_recv()
    late = [entry, swap_ig, swap_layer, mid_across]
    late += ctx_copies + mid_copies + mid_far + mid_cores + cg_copies
    for slot in range(3):
        late += sum_copies[slot]
    for copy in late:
        copy.wait_send()


def chain_call(x8, cot8, context, term, wg, wu, wd, wh):
    def sds(*shape):
        return jax.ShapeDtypeStruct(shape, BF)

    shapes = [
        sds(8, 2048), sds(8, 2048), sds(128, 256),
        sds(512, 2048), sds(512, 2048), sds(512, 2048), sds(3, 512, 896), sds(512, 256),
    ]
    dma = pltpu.SemaphoreType.DMA
    tall = lax.axis_size("in")
    depth = lax.axis_size("out") // 2
    return pl.pallas_call(
        chain_kernel,
        out_shape=shapes,
        in_specs=[VM] * 8,
        out_specs=[VM] * 8,
        scratch_shapes=[
            pltpu.VMEM((2, 8, 2048), F32),
            pltpu.VMEM((2, 16, 1024), F32),
            pltpu.VMEM((3, 128, 1024), BF),
            pltpu.VMEM((3, 128, 1024), BF),
            pltpu.VMEM((3, depth - 1, 16, 1024), BF),
            pltpu.VMEM((2, 128, 2048), BF),
            pltpu.VMEM((3, 128, 896), F32),
            pltpu.VMEM((3, 128, 896), BF),
            pltpu.VMEM((tall - 1, 3, 32, 896), BF),
            pltpu.VMEM((2, 16, 1024), F32),
            pltpu.VMEM((2, 8, 2048), F32),
            pltpu.VMEM((tall, 128, 256), BF),
            dma((2, 12)),
            dma((2, 12)),
            dma((2, 12)),
            dma((3, 2, 8)),
            dma((2, 3)),
            dma((3, 2, 3)),
            dma((2, 9)),
            dma((2, 3)),
            dma((2, 3)),
        ],
        compiler_params=pltpu.CompilerParams(
            collective_id=0, has_side_effects=True, vmem_limit_bytes=56 * 2**20
        ),
        name="chain",
    )(x8, cot8, context, term, wg, wu, wd, wh)


def positions(ids, count, share, dp, spots):
    count = count.reshape(())
    flat = jnp.where(jnp.arange(ids.shape[-1], dtype=jnp.int32) < count, spots(ids.reshape(-1)), -1)
    own = lax.dynamic_slice(flat, (dp * share,), (share,))
    pad = lambda row: jnp.pad(row, (0, 256 - row.shape[0]), constant_values=-1)
    return pad(flat), pad(own)


def local(
    inputs, context,
    gate_blocks, gate_ids, gate_count,
    up_blocks, up_ids, up_count,
    down_blocks, down_ids, down_count,
    heads_blocks, heads_ids, heads_count,
    cotangent,
):
    dp = lax.axis_index("dp")
    tall = lambda i: (i // 224) * 224 + (i % 14) * 16 + (i // 14) % 16
    pairs = [
        positions(gate_ids, gate_count, 60, dp, tall),
        positions(up_ids, up_count, 60, dp, tall),
        positions(down_ids, down_count, 60, dp, lambda i: (i % 32) * 16 + i // 32),
        positions(heads_ids, heads_count, 17, dp, lambda i: (i % 32) * 8 + i // 32),
    ]
    idx = jnp.stack([p[0] for p in pairs] + [p[1] for p in pairs])
    rows = lambda blocks: blocks.reshape(-1, CELL)
    wg, wu, wd, wh, term = place_call(
        idx, rows(gate_blocks), rows(up_blocks), rows(down_blocks), rows(heads_blocks), context
    )
    layer, input_grad, context_grad, res, cot, ig, mid, ctx = chain_call(
        inputs, cotangent, context, term, wg, wu, wd, wh
    )
    grads = grads_call(idx, res, cot, ig, mid[0], mid[1], mid[2], ctx)
    return (layer, input_grad, context_grad, *(g.reshape(1, 1, -1, CELL) for g in grads))


def solution(mesh):
    rows = P(("dp", "out"), "in")
    tall, wide = ("in", "out"), ("out", "in")

    def lists(axes):
        return P(*axes, None, None), P(*axes, None), P(*axes)

    return jax.shard_map(
        local,
        mesh=mesh,
        in_specs=(rows, P("dp", "out"), *lists(tall), *lists(tall), *lists(wide), *lists(wide), rows),
        out_specs=(
            rows,
            rows,
            P("dp", "out"),
            P(*tall, "dp", None),
            P(*tall, "dp", None),
            P(*wide, "dp", None),
            P(*wide, "dp", None),
        ),
        check_vma=False,
    )
```

```python
import jax
import jax.numpy as jnp
from jax import lax
from jax.experimental import pallas as pl
from jax.experimental.pallas import tpu as pltpu
from jax.sharding import PartitionSpec as P

BLOCK = 64
CELL = BLOCK * BLOCK
BF = jnp.bfloat16
F32 = jnp.float32
MESH = pl.DeviceIdType.MESH
VM = pl.BlockSpec(memory_space=pltpu.VMEM)
ANY = pl.BlockSpec(memory_space=pl.ANY)


def dot(a, b):
    return lax.dot_general(a, b, (((1,), (0,)), ((), ())), preferred_element_type=F32)


def dot_nt(a, b):
    return lax.dot_general(a, b, (((1,), (1,)), ((), ())), preferred_element_type=F32)


def dot_tn(a, b):
    return lax.dot_general(a, b, (((0,), (0,)), ((), ())), preferred_element_type=F32)


def one_hot(row, positions):
    spots = lax.broadcasted_iota(jnp.int32, (positions, row.shape[1]), 0)
    return jnp.where(spots == row, 1.0, 0.0).astype(BF)


def swap_matrix(inner, outer):
    rows = lax.broadcasted_iota(jnp.int32, (inner * outer, inner * outer), 0)
    cols = lax.broadcasted_iota(jnp.int32, (inner * outer, inner * outer), 1)
    source = (rows % outer) * inner + rows // outer
    return jnp.where(cols == source, 1.0, 0.0).astype(BF)


def halves(first, second):
    low = lax.broadcasted_iota(jnp.int32, first.shape, 1) < BLOCK
    return (
        jnp.where(low, first, pltpu.roll(second, BLOCK, 1)),
        jnp.where(low, pltpu.roll(first, BLOCK, 1), second),
    )


def spots(ids, count, kind):
    i = ids[...]
    if kind == "tall":
        r = (i * 2341) >> 15
        c = i - 14 * r
        spot = (r >> 4) * 224 + c * 16 + (r & 15)
    elif kind == "wide":
        spot = (i & 31) * 16 + (i >> 5)
    else:
        spot = (i & 31) * 8 + (i >> 5)
    slots = lax.broadcasted_iota(jnp.int32, i.shape, 1)
    return jnp.where(slots < count[...], spot, -1)


def place(hot, swap, blocks, stage, out, inner, used, stripes, k):
    chunk = 256 // inner
    width = out.shape[1]
    per = (width // BLOCK) * inner
    flat = dot(hot, blocks[:, k * chunk * BLOCK:(k + 1) * chunk * BLOCK]).astype(BF)
    for s in range(stripes):
        for p in range(chunk // 2):
            for q in range(width // 128):
                at = s * per + 2 * q * inner
                left = flat[at:at + inner, p * 128:(p + 1) * 128]
                right = flat[at + inner:at + 2 * inner, p * 128:(p + 1) * 128]
                pair = jnp.concatenate(halves(left, right), axis=0)
                at = s * 256 + 2 * p * inner
                stage[at:at + 2 * inner, q * 128:(q + 1) * 128] = pair
        dense = dot(swap, stage[s * 256:(s + 1) * 256, :width]).astype(BF)
        for r in range(used):
            at = s * inner * BLOCK + r * BLOCK + k * chunk
            out[at:at + chunk, :] = dense[r * chunk:(r + 1) * chunk]


def pick(left, rights, hots, outs, flats, swap, turned, inner, used, stripes):
    chunk = 256 // inner
    span = used * BLOCK
    for s in range(stripes * span // 128):
        turned[s * 128:(s + 1) * 128, :] = left[:, s * 128:(s + 1) * 128].T

    def step(k, _):
        lanes = pl.ds(pl.multiple_of(k * chunk * BLOCK, chunk * BLOCK), chunk * BLOCK)
        for s in range(stripes):
            rows = [
                turned[pl.ds(pl.multiple_of(s * span + r * BLOCK + k * chunk, 16), chunk), :]
                for r in range(used)
            ]
            rows += [jnp.zeros_like(rows[0])] * (inner - used)
            ordered = dot(swap, jnp.concatenate(rows, axis=0)).astype(BF)
            for right, flat in zip(rights, flats):
                width = right.shape[1]
                base = s * (width // BLOCK) * inner
                piece = 512 if width % 512 == 0 else 896
                for t in range(width // piece):
                    grad = dot(ordered, right[:, t * piece:(t + 1) * piece])
                    for q in range(piece // 128):
                        for p in range(chunk // 2):
                            pair = grad[2 * p * inner:(2 * p + 2) * inner, q * 128:(q + 1) * 128]
                            both = jnp.concatenate(halves(pair[:inner], pair[inner:]), axis=0)
                            at = base + (t * piece // 128 + q) * 2 * inner
                            flat[at:at + 2 * inner, p * 128:(p + 1) * 128] = both.astype(BF)
        for hot, flat, out in zip(hots, flats, outs):
            depth = hot.shape[0]
            picked = dot_tn(hot, flat[:depth, :chunk * BLOCK])
            out[:, lanes] = picked.astype(BF)
        return 0

    lax.fori_loop(0, BLOCK // chunk, step, 0)


def grads_kernel(
    gids, gcount, uids, ucount, dids, dcount, hids, hcount, res, cot, ig, mid, ctx,
    og, ou, od, oh, turned, flat_a, flat_b,
):
    swap16 = swap_matrix(16, 16)
    dp = lax.axis_index("dp")

    def hot(ids, count, kind, positions, share):
        spot = spots(ids, count, kind)
        own = spot[:, :share]
        for k in range(1, 4):
            own = jnp.where(dp == k, spot[:, k * share:(k + 1) * share], own)
        return one_hot(own, positions)

    hots = (hot(gids, gcount, "tall", 448, 60), hot(uids, ucount, "tall", 448, 60))
    pick(res, (mid.at[1], mid.at[2]), hots, (og, ou), (flat_a, flat_b), swap16, turned, 16, 16, 2)
    hots = (hot(dids, dcount, "wide", 512, 60),)
    pick(mid.at[0], (cot,), hots, (od,), (flat_a,), swap16, turned, 16, 14, 1)
    hots = (hot(hids, hcount, "heads", 256, 17),)
    pick(ctx, (ig,), hots, (oh,), (flat_a,), swap_matrix(32, 8), turned, 8, 4, 1)


def grads_call(lists, res, cot, ig, mid, ctx):
    shapes = [jax.ShapeDtypeStruct((n, CELL), BF) for n in (60, 60, 60, 17)]
    return pl.pallas_call(
        grads_kernel,
        out_shape=shapes,
        in_specs=[VM] * 13,
        out_specs=[VM] * 4,
        scratch_shapes=[
            pltpu.VMEM((2048, 512), BF),
            pltpu.VMEM((512, 2048), BF),
            pltpu.VMEM((512, 2048), BF),
        ],
        compiler_params=pltpu.CompilerParams(vmem_limit_bytes=56 * 2**20),
        name="grads",
    )(*lists, res, cot, ig, mid, ctx)


class Links:

    def __init__(self):
        self.dp, self.y, self.out = lax.axis_index("dp"), lax.axis_index("in"), lax.axis_index("out")
        self.depth = lax.axis_size("out") // 2
        self.tall = lax.axis_size("in")
        self.core, self.z = self.dp % 2, self.out // 2
        self.low = self.out % 2
        self.x = (self.dp // 2) * 2 + self.low

    def at_x(self, k):
        x = (self.x + k) % 4
        return (x // 2) * 2 + self.core, self.y, self.z * 2 + x % 2

    def at_z(self, k):
        return self.dp, self.y, ((self.z + k) % self.depth) * 2 + self.low

    def at_y(self, k):
        return self.dp, (self.y + k) % self.tall, self.out

    def sibling(self):
        return (self.dp // 2) * 2 + 1 - self.core, self.y, self.out

    def beside(self):
        return self.dp, self.y, self.z * 2 + 1 - self.low

    def across(self):
        return (self.dp + 2) % 4, self.y, self.out

    def greet(self):
        barrier = pltpu.get_barrier_semaphore()
        peers = [self.at_x(k) for k in (1, 2, 3)]
        peers += [self.at_z(k) for k in range(1, self.depth)]
        peers += [self.at_y(k) for k in range(1, self.tall)]
        peers += [self.sibling()]
        for peer in peers:
            pl.semaphore_signal(barrier, inc=1, device_id=peer, device_id_type=MESH)
        return barrier, len(peers)

    def meet(self, greeted):
        pl.semaphore_wait(*greeted)


def send(source, target, sems, k, to):
    copy = pltpu.make_async_remote_copy(
        src_ref=source,
        dst_ref=target,
        send_sem=sems.at[0, k],
        recv_sem=sems.at[1, k],
        device_id=to,
        device_id_type=MESH,
    )
    copy.start()
    return copy


class Spread:

    def __init__(self, me, whole, sems):
        self.me, self.whole, self.sems = me, whole, sems
        self.home = pl.ds(pl.multiple_of(me.low * 1024, 1024), 1024)
        self.away = pl.ds(pl.multiple_of((1 - me.low) * 1024, 1024), 1024)
        self.other = (me.dp + 2) % 4
        self.far = me.at_x(jnp.where(me.low == 0, 3, 1))
        self.sent = []

    def rows(self, dp, start=0, size=128):
        return pl.ds(pl.multiple_of(dp * 128 + start, 16), size)

    def move(self, rows, lanes, k, to):
        spot = self.whole.at[rows, lanes]
        copy = send(spot, spot, self.sems, k, to)
        self.sent.append(copy)
        return copy

    def chunk(self, z):
        return pl.ds(pl.multiple_of(self.me.dp * 128 + (z % self.me.depth) * 16, 16), 16)

    def over_z(self, own):
        me = self.me
        self.whole[self.chunk(me.z), self.home] = own
        self.first = {k: self.move(self.chunk(me.z), self.home, k, me.at_z(k)) for k in range(1, me.depth)}

    def over_x(self):
        me, depth = self.me, self.me.depth
        self.near = [self.move(self.chunk(me.z), self.home, 8, me.beside())]
        for k in sorted(range(1, depth), key=lambda k: min(k, depth - k)):
            self.first[k].wait_recv()
            self.near.append(self.move(self.chunk(me.z + depth - k), self.home, 8 + k, me.beside()))
        self.wide = self.move(self.rows(me.dp), self.home, 16, self.far)

    def group(self):
        for copy in self.near:
            copy.wait_recv()
        return self.rows(self.me.dp)

    def forward(self):
        me = self.me
        self.half_a = self.move(self.rows(me.dp, 0, 64), self.away, 17, self.far)
        self.cores = [self.move(self.rows(me.dp), slice(None), 19, me.sibling())]
        self.wide.wait_recv()
        self.half_b = self.move(self.rows(self.other, 64, 64), self.away, 18, me.beside())

    def over_cores(self):
        self.half_a.wait_recv()
        self.half_b.wait_recv()
        self.cores.append(self.move(self.rows(self.other), slice(None), 20, self.me.sibling()))

    def finish(self):
        for copy in self.cores:
            copy.wait_recv()

    def drain(self):
        for copy in self.sent:
            copy.wait_send()


class Collect:

    def __init__(self, me, term, half, sums, parts, sems):
        self.me, self.term, self.half, self.sums, self.parts, self.sems = me, term, half, sums, parts, sems
        self.order = sorted(range(me.depth), key=lambda k: -min(k, me.depth - k))

    def chunk(self, k):
        return pl.ds(pl.multiple_of(((self.me.z + k) % self.me.depth) * 16, 16), 16)

    def over_x(self):
        away = pl.ds(pl.multiple_of((1 - self.me.low) * 1024, 1024), 1024)
        self.near = {}
        for k in self.order:
            rows = self.chunk(k)
            self.near[k] = send(self.term.at[rows, away], self.half.at[rows, :], self.sems, 8 + k, self.me.beside())

    def over_z(self):
        me = self.me
        home = pl.ds(pl.multiple_of(me.low * 1024, 1024), 1024)
        self.far = {}
        for k in self.order:
            rows = self.chunk(k)
            self.near[k].wait_recv()
            both = self.term[rows, home].astype(F32) + self.half[rows, :].astype(F32)
            if k == 0:
                self.own = both
            else:
                self.sums[rows, :] = both.astype(BF)
                self.far[k] = send(self.sums.at[rows, :], self.parts.at[k - 1], self.sems, k, me.at_z(k))

    def total(self):
        total = self.own
        for k in reversed(self.order[:-1]):
            self.far[k].wait_recv()
            total = total + self.parts[k - 1].astype(F32)
        return total

    def drain(self):
        for copy in list(self.near.values()) + list(self.far.values()):
            copy.wait_send()


def swap_out(me, total, outgoing, landing, sems, k):
    outgoing[...] = total
    away = outgoing.at[pl.ds(pl.multiple_of((1 - me.low) * 8, 8), 8), :]
    lanes = pl.ds(pl.multiple_of(me.low * 1024, 1024), 1024)
    landing[:, lanes] = outgoing[pl.ds(pl.multiple_of(me.low * 8, 8), 8), :]
    return send(away, landing.at[:, lanes], sems, k, me.beside())


def chain_kernel(
    x8, cot8, context, gids, gcount, uids, ucount, dids, dcount, hids, hcount, gate, up, down, heads,
    layer, input_grad, context_grad, res, cot, ig, mid, ctx,
    gate_in, up_in, down_in, stage, wg, wu, wd, wh, term,
    cells, edge, halves_in, sums, parts, backs,
    shares, shares_bf, gathered, swap_from, swap_to, near_sums,
    sem_in, sem_res, sem_cot, sem_ig, sem_rs, sem_ctx, sem_sum, sem_mid, sem_cg, sem_swap,
):
    loads = []
    for k, (source, target) in enumerate(((gate, gate_in), (up, up_in), (down, down_in))):
        loads.append(pltpu.make_async_copy(source, target, sem_in.at[k]))
        loads[-1].start()
    me = Links()
    greeted = me.greet()
    hot = one_hot(spots(hids, hcount, "heads"), 256)
    swap = swap_matrix(8, 32)
    for k in range(2):
        place(hot, swap, heads, stage, wh, 8, 4, 1, k)
    for t in range(2):
        cols = slice(t * 1024, (t + 1) * 1024)
        term[:, cols] = dot(context[...], wh[:, cols]).astype(BF)

    swap16 = swap_matrix(16, 16)
    work = []

    def queue(load, ids, count, kind, blocks, out, stripes, used):
        held = {}

        def step(k):
            if k == 0:
                loads[load].wait()
                held["hot"] = one_hot(spots(ids, count, kind), 448 if kind == "tall" else 512)
            place(held["hot"], swap16, blocks, stage, out, 16, used, stripes, k)

        for k in range(4):
            work.append(lambda k=k: step(k))

    queue(0, gids, gcount, "tall", gate_in, wg, 2, 16)
    queue(1, uids, ucount, "tall", up_in, wu, 2, 16)
    queue(2, dids, dcount, "wide", down_in, wd, 1, 14)

    def fill(n):
        for _ in range(n):
            work.pop(0)()

    low8 = pl.ds(pl.multiple_of(me.low * 8, 8), 8)
    away = pl.ds(pl.multiple_of((1 - me.low) * 1024, 1024), 1024)
    home = pl.ds(pl.multiple_of(me.low * 1024, 1024), 1024)

    def collect(term, k):
        return Collect(me, term, halves_in.at[k], sums.at[k], parts.at[k], sem_rs.at[k])

    cells[0] = x8[...].astype(F32)
    cells[1] = cot8[...].astype(F32)
    edge[:, low8, :] = cells[:, :, home]
    me.meet(greeted)
    attention = collect(term, 0)
    attention.over_x()
    entry = send(cells.at[:, :, away], edge.at[:, low8, :], sem_swap, 0, me.beside())
    fill(3)
    attention.over_z()
    entry.wait_recv()
    spread_cot = Spread(me, cot, sem_cot)
    spread_cot.over_z(edge[1].astype(BF))
    own_ctx = pl.ds(pl.multiple_of(me.dp * 128, 128), 128)
    ctx[own_ctx, :] = context[...]
    spot = ctx.at[own_ctx, :]
    ctx_copies = [send(spot, spot, sem_ctx, k, to) for k, to in enumerate((me.sibling(), me.across()))]
    fill(3)
    residual = edge[0] + attention.total()
    spread_res = Spread(me, res, sem_res)
    spread_res.over_z(residual.astype(BF))
    spread_cot.over_x()
    fill(2)
    spread_res.over_x()
    fill(4)

    def share(slot):
        copies = []
        for k in range(1, me.tall):
            rows = pl.ds(pl.multiple_of(((me.y + k) % me.tall) * 32, 32), 32)
            copies.append(
                send(shares_bf.at[slot, rows, :], gathered.at[k - 1, slot], sem_sum.at[slot], k - 1, me.at_y(k))
            )
        return copies

    rows = spread_cot.group()
    for t in range(2):
        lanes = slice(t * 512, min(896, (t + 1) * 512))
        shares[2, :, lanes] = dot_nt(cot[rows, :], wd[lanes, :])
    shares_bf[2] = shares[2].astype(BF)
    sum_copies = {2: share(2)}

    rows = spread_res.group()
    for slot, weight in ((0, wg), (1, wu)):
        shares[slot] = dot(res[rows, :], weight[...])
        shares_bf[slot] = shares[slot].astype(BF)
        sum_copies[slot] = share(slot)

    spread_cot.forward()
    quarter = pl.ds(pl.multiple_of(me.y * 32, 32), 32)

    def total_of(slot):
        total = shares[slot, quarter, :]
        for k in range(me.tall - 1):
            sum_copies[slot][k].wait_recv()
            total = total + gathered[k, slot].astype(F32)
        return total

    hidden_grad = total_of(2)
    gate_sum = total_of(0)
    sigmoid = 1.0 / (1.0 + jnp.exp(-gate_sum))
    slope = hidden_grad * sigmoid * (1.0 + gate_sum * (1.0 - sigmoid))
    swish = gate_sum * sigmoid
    up_sum = total_of(1)
    spot_rows = pl.ds(pl.multiple_of(me.dp * 128 + me.y * 32, 32), 32)
    mid[1, spot_rows, :] = (slope * up_sum).astype(BF)
    mid[2, spot_rows, :] = (hidden_grad * swish).astype(BF)
    spot = mid.at[pl.ds(1, 2), spot_rows, :]
    mid_deltas = [send(spot, spot, sem_mid, k - 1, me.at_y(k)) for k in range(1, me.tall)]
    mid[0, spot_rows, :] = (swish * up_sum).astype(BF)
    spot = mid.at[0, spot_rows, :]
    mid_hidden = [send(spot, spot, sem_mid, 2 + k, me.at_y(k)) for k in range(1, me.tall)]
    spot = mid.at[:, spot_rows, :]
    mid_across = send(spot, spot, sem_mid, 6, me.across())
    spread_res.forward()
    for copy in mid_deltas:
        copy.wait_recv()

    rows = pl.ds(pl.multiple_of(me.dp * 128, 128), 128)
    for t in range(4):
        lanes = slice(t * 512, (t + 1) * 512)
        backs[0, :, lanes] = (
            dot_nt(mid[1, rows, :], wg[lanes, :]) + dot_nt(mid[2, rows, :], wu[lanes, :])
        ).astype(BF)
    backward = collect(backs.at[0], 1)
    backward.over_x()
    for copy in mid_hidden:
        copy.wait_recv()
    for t in range(2):
        lanes = slice(t * 1024, (t + 1) * 1024)
        backs[1, :, lanes] = dot(mid[0, rows, :], wd[:, lanes]).astype(BF)
    backward.over_z()
    forward = collect(backs.at[1], 2)
    forward.over_x()

    mid_across.wait_recv()
    spot = mid.at[:, pl.ds(pl.multiple_of(((me.dp + 2) % 4) * 128 + me.y * 32, 32), 32), :]
    mid_far = [send(spot, spot, sem_mid, 6 + k, me.at_y(k)) for k in range(1, me.tall)]
    spread_cot.over_cores()
    spread_res.over_cores()

    total = edge[1] + backward.total()
    spread_ig = Spread(me, ig, sem_ig)
    spread_ig.over_z(total.astype(BF))
    swap_ig = swap_out(me, total, swap_from.at[0], swap_to.at[0], sem_swap, 1)
    forward.over_z()
    spread_ig.over_x()

    for copy in mid_far:
        copy.wait_recv()
    mid_cores = []
    for k, dp in enumerate((me.dp, (me.dp + 2) % 4)):
        spot = mid.at[:, pl.ds(pl.multiple_of(dp * 128, 128), 128), :]
        mid_cores.append(send(spot, spot, sem_mid, 10 + k, me.sibling()))

    rows = spread_ig.group()
    near_sums[me.y] = dot_nt(ig[rows, :], wh[...]).astype(BF)
    spot = near_sums.at[me.y]
    cg_copies = [send(spot, spot, sem_cg, k - 1, me.at_y(k)) for k in range(1, me.tall)]
    spread_ig.forward()

    total = residual.astype(BF).astype(F32) + forward.total()
    swap_layer = swap_out(me, total, swap_from.at[1], swap_to.at[1], sem_swap, 2)
    ctx_copies[1].wait_recv()
    spot = ctx.at[pl.ds(pl.multiple_of(((me.dp + 2) % 4) * 128, 128), 128), :]
    ctx_copies.append(send(spot, spot, sem_ctx, 2, me.sibling()))
    swap_ig.wait_recv()
    input_grad[...] = swap_to[0].astype(BF)
    spread_ig.over_cores()

    for copy in cg_copies:
        copy.wait_recv()
    total = near_sums[0].astype(F32)
    for k in range(1, me.tall):
        total = total + near_sums[k].astype(F32)
    context_grad[...] = total.astype(BF)
    swap_layer.wait_recv()
    layer[...] = swap_to[1].astype(BF)

    for spread in (spread_cot, spread_res, spread_ig):
        spread.finish()
    for copy in mid_cores + [ctx_copies[0], ctx_copies[2]]:
        copy.wait_recv()
    for part in (spread_cot, spread_res, spread_ig, attention, backward, forward):
        part.drain()
    late = [entry, swap_ig, swap_layer, mid_across]
    late += ctx_copies + mid_deltas + mid_hidden + mid_far + mid_cores + cg_copies
    for slot in range(3):
        late += sum_copies[slot]
    for copy in late:
        copy.wait_send()


def chain_call(x8, cot8, context, lists, gate, up, down, heads):
    def sds(*shape):
        return jax.ShapeDtypeStruct(shape, BF)

    shapes = [
        sds(8, 2048), sds(8, 2048), sds(128, 256),
        sds(512, 2048), sds(512, 2048), sds(512, 2048), sds(3, 512, 896), sds(512, 256),
    ]
    dma = pltpu.SemaphoreType.DMA
    tall = lax.axis_size("in")
    depth = lax.axis_size("out") // 2
    return pl.pallas_call(
        chain_kernel,
        out_shape=shapes,
        in_specs=[VM] * 11 + [ANY] * 3 + [VM],
        out_specs=[VM] * 8,
        scratch_shapes=[
            pltpu.VMEM((240, CELL), BF),
            pltpu.VMEM((240, CELL), BF),
            pltpu.VMEM((240, CELL), BF),
            pltpu.VMEM((512, 2048), BF),
            pltpu.VMEM((2048, 896), BF),
            pltpu.VMEM((2048, 896), BF),
            pltpu.VMEM((896, 2048), BF),
            pltpu.VMEM((256, 2048), BF),
            pltpu.VMEM((128, 2048), BF),
            pltpu.VMEM((2, 8, 2048), F32),
            pltpu.VMEM((2, 16, 1024), F32),
            pltpu.VMEM((3, 128, 1024), BF),
            pltpu.VMEM((3, 128, 1024), BF),
            pltpu.VMEM((3, depth - 1, 16, 1024), BF),
            pltpu.VMEM((2, 128, 2048), BF),
            pltpu.VMEM((3, 128, 896), F32),
            pltpu.VMEM((3, 128, 896), BF),
            pltpu.VMEM((tall - 1, 3, 32, 896), BF),
            pltpu.VMEM((2, 16, 1024), F32),
            pltpu.VMEM((2, 8, 2048), F32),
            pltpu.VMEM((tall, 128, 256), BF),
            dma((3,)),
            dma((2, 21)),
            dma((2, 21)),
            dma((2, 21)),
            dma((3, 2, 16)),
            dma((2, 3)),
            dma((3, 2, 3)),
            dma((2, 12)),
            dma((2, 3)),
            dma((2, 3)),
        ],
        compiler_params=pltpu.CompilerParams(
            collective_id=0, has_side_effects=True, vmem_limit_bytes=58 * 2**20
        ),
        name="chain",
    )(x8, cot8, context, *lists, gate, up, down, heads)


def local(
    inputs, context,
    gate_blocks, gate_ids, gate_count,
    up_blocks, up_ids, up_count,
    down_blocks, down_ids, down_count,
    heads_blocks, heads_ids, heads_count,
    cotangent,
):
    rows = lambda blocks: blocks.reshape(-1, CELL)
    line = lambda ids: ids.reshape(1, -1)
    lists = (
        line(gate_ids), gate_count, line(up_ids), up_count,
        line(down_ids), down_count, line(heads_ids), heads_count,
    )
    layer, input_grad, context_grad, res, cot, ig, mid, ctx = chain_call(
        inputs, cotangent, context, lists,
        rows(gate_blocks), rows(up_blocks), rows(down_blocks), rows(heads_blocks),
    )
    grads = grads_call(lists, res, cot, ig, mid, ctx)
    return (layer, input_grad, context_grad, *(g.reshape(1, 1, -1, CELL) for g in grads))


def solution(mesh):
    rows = P(("dp", "out"), "in")
    tall, wide = ("in", "out"), ("out", "in")

    def lists(axes):
        return P(*axes, None, None), P(*axes, None), P(*axes)

    return jax.shard_map(
        local,
        mesh=mesh,
        in_specs=(rows, P("dp", "out"), *lists(tall), *lists(tall), *lists(wide), *lists(wide), rows),
        out_specs=(
            rows,
            rows,
            P("dp", "out"),
            P(*tall, "dp", None),
            P(*tall, "dp", None),
            P(*wide, "dp", None),
            P(*wide, "dp", None),
        ),
        check_vma=False,
    )
```

```python
import jax
import jax.numpy as jnp
from jax import lax
from jax.experimental import pallas as pl
from jax.experimental.pallas import tpu as pltpu
from jax.sharding import PartitionSpec as P

BLOCK = 64
CELL = BLOCK * BLOCK
BF = jnp.bfloat16
F32 = jnp.float32
MESH = pl.DeviceIdType.MESH
VM = pl.BlockSpec(memory_space=pltpu.VMEM)
ANY = pl.BlockSpec(memory_space=pl.ANY)


def dot(a, b):
    return lax.dot_general(a, b, (((1,), (0,)), ((), ())), preferred_element_type=F32)


def dot_nt(a, b):
    return lax.dot_general(a, b, (((1,), (1,)), ((), ())), preferred_element_type=F32)


def dot_tn(a, b):
    return lax.dot_general(a, b, (((0,), (0,)), ((), ())), preferred_element_type=F32)


def one_hot(row, positions):
    spots = lax.broadcasted_iota(jnp.int32, (positions, row.shape[1]), 0)
    return jnp.where(spots == row, 1.0, 0.0).astype(BF)


def swap_matrix(inner, outer):
    rows = lax.broadcasted_iota(jnp.int32, (inner * outer, inner * outer), 0)
    cols = lax.broadcasted_iota(jnp.int32, (inner * outer, inner * outer), 1)
    source = (rows % outer) * inner + rows // outer
    return jnp.where(cols == source, 1.0, 0.0).astype(BF)


def halves(first, second):
    low = lax.broadcasted_iota(jnp.int32, first.shape, 1) < BLOCK
    return (
        jnp.where(low, first, pltpu.roll(second, BLOCK, 1)),
        jnp.where(low, pltpu.roll(first, BLOCK, 1), second),
    )


def spots(ids, count, kind):
    i = ids[...]
    if kind == "tall":
        r = (i * 2341) >> 15
        c = i - 14 * r
        spot = (r >> 4) * 224 + c * 16 + (r & 15)
    elif kind == "wide":
        spot = (i & 31) * 16 + (i >> 5)
    else:
        spot = (i & 31) * 8 + (i >> 5)
    slots = lax.broadcasted_iota(jnp.int32, i.shape, 1)
    return jnp.where(slots < count[...], spot, -1)


def place(hot, swap, blocks, stage, out, inner, used, stripes, k):
    chunk = 256 // inner
    width = out.shape[1]
    per = (width // BLOCK) * inner
    flat = dot(hot, blocks[:, k * chunk * BLOCK:(k + 1) * chunk * BLOCK]).astype(BF)
    for s in range(stripes):
        for p in range(chunk // 2):
            for q in range(width // 128):
                at = s * per + 2 * q * inner
                left = flat[at:at + inner, p * 128:(p + 1) * 128]
                right = flat[at + inner:at + 2 * inner, p * 128:(p + 1) * 128]
                pair = jnp.concatenate(halves(left, right), axis=0)
                at = s * 256 + 2 * p * inner
                stage[at:at + 2 * inner, q * 128:(q + 1) * 128] = pair
        dense = dot(swap, stage[s * 256:(s + 1) * 256, :width]).astype(BF)
        for r in range(used):
            at = s * inner * BLOCK + r * BLOCK + k * chunk
            out[at:at + chunk, :] = dense[r * chunk:(r + 1) * chunk]


def turn(left, turned, start, stop):
    for s in range(start, stop):
        turned[s * 128:(s + 1) * 128, :] = left[:, s * 128:(s + 1) * 128].T


def order(turned, swap, ordered, inner, used, stripes, k):
    chunk = 256 // inner
    for s in range(stripes):
        rows = [
            turned[s * used * BLOCK + r * BLOCK + k * chunk:s * used * BLOCK + r * BLOCK + (k + 1) * chunk, :]
            for r in range(used)
        ]
        rows += [jnp.zeros_like(rows[0])] * (inner - used)
        ordered[s * 256:(s + 1) * 256, :] = dot(swap, jnp.concatenate(rows, axis=0)).astype(BF)


def pick(ordered, right, hot, out, flat, inner, stripes, k):
    chunk = 256 // inner
    width = right.shape[1]
    piece = 1024 if width % 1024 == 0 else width
    for s in range(stripes):
        base = s * (width // BLOCK) * inner
        for t in range(width // piece):
            grad = dot(ordered[s * 256:(s + 1) * 256, :], right[:, t * piece:(t + 1) * piece]).astype(BF)
            for q in range(piece // 128):
                for p in range(chunk // 2):
                    pair = grad[2 * p * inner:(2 * p + 2) * inner, q * 128:(q + 1) * 128]
                    both = jnp.concatenate(halves(pair[:inner], pair[inner:]), axis=0)
                    at = base + (t * piece // 128 + q) * 2 * inner
                    flat[at:at + 2 * inner, p * 128:(p + 1) * 128] = both
    picked = dot_tn(hot, flat[:hot.shape[0], :chunk * BLOCK])
    out[:, k * chunk * BLOCK:(k + 1) * chunk * BLOCK] = picked.astype(BF)


def own_hot(ids, count, kind, positions, share, slots, dp):
    spot = spots(ids, count, kind)
    if slots > share:
        spot = jnp.concatenate([spot, jnp.full((1, slots - share), -1, jnp.int32)], axis=1)
    own = spot[:, :slots]
    for k in range(1, 4):
        own = jnp.where(dp == k, spot[:, k * share:k * share + slots], own)
    lanes = lax.broadcasted_iota(jnp.int32, own.shape, 1)
    return one_hot(jnp.where(lanes < share, own, -1), positions)


def finish_kernel(
    hids, hcount, ctx, ig, layer, input_grad, context_grad, og, ou, od,
    layer_to, input_grad_to, context_grad_to, og_to, ou_to, od_to, oh, turned, ordered, flat, sems,
):
    copies = []
    pairs = ((og, og_to), (ou, ou_to), (od, od_to), (layer, layer_to), (input_grad, input_grad_to))
    for k, (source, target) in enumerate(pairs + ((context_grad, context_grad_to),)):
        if source.shape != target.shape:
            source = source.at[:target.shape[0], :]
        copies.append(pltpu.make_async_copy(source, target, sems.at[k]))
        copies[-1].start()
    hot = own_hot(hids, hcount, "heads", 256, 17, 17, lax.axis_index("dp"))
    swap = swap_matrix(32, 8)
    turn(ctx, turned, 0, 2)
    for k in range(2):
        order(turned, swap, ordered, 8, 4, 1, k)
        pick(ordered, ig, hot, oh, flat, 8, 1, k)
    for copy in copies:
        copy.wait()


def finish_call(hids, hcount, ctx, ig, *results):
    shapes = [jax.ShapeDtypeStruct(r.shape, BF) for r in results]
    shapes.append(jax.ShapeDtypeStruct((17, CELL), BF))
    return pl.pallas_call(
        finish_kernel,
        out_shape=shapes,
        in_specs=[VM] * 4 + [ANY] * 6,
        out_specs=[ANY] * 6 + [VM],
        scratch_shapes=[
            pltpu.VMEM((256, 512), BF),
            pltpu.VMEM((256, 512), BF),
            pltpu.VMEM((256, 2048), BF),
            pltpu.SemaphoreType.DMA((6,)),
        ],
        compiler_params=pltpu.CompilerParams(vmem_limit_bytes=56 * 2**20),
        name="finish",
    )(hids, hcount, ctx, ig, *results)


class Links:

    def __init__(self):
        self.dp, self.y, self.out = lax.axis_index("dp"), lax.axis_index("in"), lax.axis_index("out")
        self.depth = lax.axis_size("out") // 2
        self.tall = lax.axis_size("in")
        self.core, self.z = self.dp % 2, self.out // 2
        self.low = self.out % 2
        self.x = (self.dp // 2) * 2 + self.low

    def at_x(self, k):
        x = (self.x + k) % 4
        return (x // 2) * 2 + self.core, self.y, self.z * 2 + x % 2

    def at_z(self, k):
        return self.dp, self.y, ((self.z + k) % self.depth) * 2 + self.low

    def at_y(self, k):
        return self.dp, (self.y + k) % self.tall, self.out

    def sibling(self):
        return (self.dp // 2) * 2 + 1 - self.core, self.y, self.out

    def beside(self):
        return self.dp, self.y, self.z * 2 + 1 - self.low

    def across(self):
        return (self.dp + 2) % 4, self.y, self.out

    def greet(self):
        barrier = pltpu.get_barrier_semaphore()
        peers = [self.at_x(k) for k in (1, 2, 3)]
        peers += [self.at_z(k) for k in range(1, self.depth)]
        peers += [self.at_y(k) for k in range(1, self.tall)]
        peers += [self.sibling()]
        for peer in peers:
            pl.semaphore_signal(barrier, inc=1, device_id=peer, device_id_type=MESH)
        return barrier, len(peers)

    def meet(self, greeted):
        pl.semaphore_wait(*greeted)


def send(source, target, sems, k, to):
    copy = pltpu.make_async_remote_copy(
        src_ref=source,
        dst_ref=target,
        send_sem=sems.at[0, k],
        recv_sem=sems.at[1, k],
        device_id=to,
        device_id_type=MESH,
    )
    copy.start()
    return copy


class Spread:

    def __init__(self, me, whole, sems):
        self.me, self.whole, self.sems = me, whole, sems
        self.home = pl.ds(pl.multiple_of(me.low * 1024, 1024), 1024)
        self.away = pl.ds(pl.multiple_of((1 - me.low) * 1024, 1024), 1024)
        self.other = (me.dp + 2) % 4
        self.far = me.at_x(jnp.where(me.low == 0, 3, 1))
        self.sent = []

    def rows(self, dp, start=0, size=128):
        return pl.ds(pl.multiple_of(dp * 128 + start, 16), size)

    def move(self, rows, lanes, k, to):
        spot = self.whole.at[rows, lanes]
        copy = send(spot, spot, self.sems, k, to)
        self.sent.append(copy)
        return copy

    def chunk(self, z):
        return pl.ds(pl.multiple_of(self.me.dp * 128 + (z % self.me.depth) * 16, 16), 16)

    def over_z(self, own):
        me = self.me
        self.whole[self.chunk(me.z), self.home] = own
        self.first = {k: self.move(self.chunk(me.z), self.home, k, me.at_z(k)) for k in range(1, me.depth)}

    def over_x(self, between=None):
        me, depth = self.me, self.me.depth
        self.near = [self.move(self.chunk(me.z), self.home, 8, me.beside())]
        for k in sorted(range(1, depth), key=lambda k: min(k, depth - k)):
            if between is not None and k < depth - k + 1:
                between(1)
            self.first[k].wait_recv()
            self.near.append(self.move(self.chunk(me.z + depth - k), self.home, 8 + k, me.beside()))
        self.wide = self.move(self.rows(me.dp), self.home, 16, self.far)

    def group(self):
        for copy in self.near:
            copy.wait_recv()
        return self.rows(self.me.dp)

    def forward(self):
        me = self.me
        self.half_a = self.move(self.rows(me.dp, 0, 64), self.away, 17, self.far)
        self.cores = [self.move(self.rows(me.dp), slice(None), 19, me.sibling())]
        self.wide.wait_recv()
        self.half_b = self.move(self.rows(self.other, 64, 64), self.away, 18, me.beside())

    def over_cores(self):
        self.half_a.wait_recv()
        self.half_b.wait_recv()
        self.cores.append(self.move(self.rows(self.other), slice(None), 20, self.me.sibling()))

    def finish(self):
        for copy in self.cores:
            copy.wait_recv()

    def drain(self):
        for copy in self.sent:
            copy.wait_send()


class Collect:

    def __init__(self, me, term, half, sums, parts, sems):
        self.me, self.term, self.half, self.sums, self.parts, self.sems = me, term, half, sums, parts, sems
        self.order = sorted(range(me.depth), key=lambda k: -min(k, me.depth - k))

    def chunk(self, k):
        return pl.ds(pl.multiple_of(((self.me.z + k) % self.me.depth) * 16, 16), 16)

    def over_x(self):
        away = pl.ds(pl.multiple_of((1 - self.me.low) * 1024, 1024), 1024)
        self.near = {}
        for k in self.order:
            rows = self.chunk(k)
            self.near[k] = send(self.term.at[rows, away], self.half.at[rows, :], self.sems, 8 + k, self.me.beside())

    def over_z(self):
        me = self.me
        home = pl.ds(pl.multiple_of(me.low * 1024, 1024), 1024)
        self.far = {}
        for k in self.order:
            rows = self.chunk(k)
            self.near[k].wait_recv()
            both = self.term[rows, home].astype(F32) + self.half[rows, :].astype(F32)
            if k == 0:
                self.own = both
            else:
                self.sums[rows, :] = both.astype(BF)
                self.far[k] = send(self.sums.at[rows, :], self.parts.at[k - 1], self.sems, k, me.at_z(k))

    def total(self):
        total = self.own
        for k in reversed(self.order[:-1]):
            self.far[k].wait_recv()
            total = total + self.parts[k - 1].astype(F32)
        return total

    def drain(self):
        for copy in list(self.near.values()) + list(self.far.values()):
            copy.wait_send()


def swap_out(me, total, outgoing, landing, sems, k):
    outgoing[...] = total
    away = outgoing.at[pl.ds(pl.multiple_of((1 - me.low) * 8, 8), 8), :]
    lanes = pl.ds(pl.multiple_of(me.low * 1024, 1024), 1024)
    landing[:, lanes] = outgoing[pl.ds(pl.multiple_of(me.low * 8, 8), 8), :]
    return send(away, landing.at[:, lanes], sems, k, me.beside())


def chain_kernel(
    x8, cot8, context, gids, gcount, uids, ucount, dids, dcount, hids, hcount, gate, up, down, heads,
    layer, input_grad, context_grad, og, ou, od, ig, ctx,
    res, cot, mid, turned, ordered, flat, gate_in, up_in, down_in, stage, wg, wu, wd, wh, term,
    cells, edge, halves_in, sums, parts, backs,
    shares, shares_bf, gathered, swap_from, swap_to, near_sums,
    sem_in, sem_res, sem_cot, sem_ig, sem_rs, sem_ctx, sem_sum, sem_mid, sem_cg, sem_swap,
):
    loads = []
    for k, (source, target) in enumerate(((gate, gate_in), (up, up_in), (down, down_in))):
        loads.append(pltpu.make_async_copy(source, target, sem_in.at[k]))
        loads[-1].start()
    me = Links()
    greeted = me.greet()
    hot = one_hot(spots(hids, hcount, "heads"), 256)
    swap = swap_matrix(8, 32)
    for k in range(2):
        place(hot, swap, heads, stage, wh, 8, 4, 1, k)
    for t in range(2):
        cols = slice(t * 1024, (t + 1) * 1024)
        term[:, cols] = dot(context[...], wh[:, cols]).astype(BF)

    swap16 = swap_matrix(16, 16)
    work = []

    def queue(load, ids, count, kind, blocks, out, stripes, used):
        held = {}

        def step(k):
            if k == 0:
                loads[load].wait()
                held["hot"] = one_hot(spots(ids, count, kind), 448 if kind == "tall" else 512)
            place(held["hot"], swap16, blocks, stage, out, 16, used, stripes, k)

        for k in range(4):
            work.append(lambda k=k: step(k))

    queue(0, gids, gcount, "tall", gate_in, wg, 2, 16)
    queue(1, uids, ucount, "tall", up_in, wu, 2, 16)
    queue(2, dids, dcount, "wide", down_in, wd, 1, 14)

    def fill(n):
        for _ in range(n):
            work.pop(0)()

    low8 = pl.ds(pl.multiple_of(me.low * 8, 8), 8)
    away = pl.ds(pl.multiple_of((1 - me.low) * 1024, 1024), 1024)
    home = pl.ds(pl.multiple_of(me.low * 1024, 1024), 1024)

    def collect(term, k):
        return Collect(me, term, halves_in.at[k], sums.at[k], parts.at[k], sem_rs.at[k])

    cells[0] = x8[...].astype(F32)
    cells[1] = cot8[...].astype(F32)
    edge[:, low8, :] = cells[:, :, home]
    me.meet(greeted)
    attention = collect(term, 0)
    attention.over_x()
    entry = send(cells.at[:, :, away], edge.at[:, low8, :], sem_swap, 0, me.beside())
    fill(3)
    attention.over_z()
    entry.wait_recv()
    spread_cot = Spread(me, cot, sem_cot)
    spread_cot.over_z(edge[1].astype(BF))
    own_ctx = pl.ds(pl.multiple_of(me.dp * 128, 128), 128)
    ctx[own_ctx, :] = context[...]
    spot = ctx.at[own_ctx, :]
    ctx_copies = [send(spot, spot, sem_ctx, k, to) for k, to in enumerate((me.sibling(), me.across()))]
    fill(3)
    residual = edge[0] + attention.total()
    spread_res = Spread(me, res, sem_res)
    spread_res.over_z(residual.astype(BF))
    spread_cot.over_x()
    fill(2)
    spread_res.over_x()
    fill(4)

    def share(slot):
        copies = []
        for k in range(1, me.tall):
            rows = pl.ds(pl.multiple_of(((me.y + k) % me.tall) * 32, 32), 32)
            copies.append(
                send(shares_bf.at[slot, rows, :], gathered.at[k - 1, slot], sem_sum.at[slot], k - 1, me.at_y(k))
            )
        return copies

    rows = spread_cot.group()
    for t in range(2):
        lanes = slice(t * 512, min(896, (t + 1) * 512))
        shares[2, :, lanes] = dot_nt(cot[rows, :], wd[lanes, :])
    shares_bf[2] = shares[2].astype(BF)
    sum_copies = {2: share(2)}

    rows = spread_res.group()
    for slot, weight in ((0, wg), (1, wu)):
        shares[slot] = dot(res[rows, :], weight[...])
        shares_bf[slot] = shares[slot].astype(BF)
        sum_copies[slot] = share(slot)

    spread_cot.forward()
    quarter = pl.ds(pl.multiple_of(me.y * 32, 32), 32)

    def total_of(slot):
        total = shares[slot, quarter, :]
        for k in range(me.tall - 1):
            sum_copies[slot][k].wait_recv()
            total = total + gathered[k, slot].astype(F32)
        return total

    hidden_grad = total_of(2)
    gate_sum = total_of(0)
    sigmoid = 1.0 / (1.0 + jnp.exp(-gate_sum))
    slope = hidden_grad * sigmoid * (1.0 + gate_sum * (1.0 - sigmoid))
    swish = gate_sum * sigmoid
    up_sum = total_of(1)
    spot_rows = pl.ds(pl.multiple_of(me.dp * 128 + me.y * 32, 32), 32)
    mid[1, spot_rows, :] = (slope * up_sum).astype(BF)
    mid[2, spot_rows, :] = (hidden_grad * swish).astype(BF)
    spot = mid.at[pl.ds(1, 2), spot_rows, :]
    mid_deltas = [send(spot, spot, sem_mid, k - 1, me.at_y(k)) for k in range(1, me.tall)]
    mid[0, spot_rows, :] = (swish * up_sum).astype(BF)
    spot = mid.at[0, spot_rows, :]
    mid_hidden = [send(spot, spot, sem_mid, 2 + k, me.at_y(k)) for k in range(1, me.tall)]
    spot = mid.at[:, spot_rows, :]
    mid_across = send(spot, spot, sem_mid, 6, me.across())
    spread_res.forward()
    for copy in mid_deltas:
        copy.wait_recv()

    rows = pl.ds(pl.multiple_of(me.dp * 128, 128), 128)
    for t in range(4):
        lanes = slice(t * 512, (t + 1) * 512)
        backs[0, :, lanes] = (
            dot_nt(mid[1, rows, :], wg[lanes, :]) + dot_nt(mid[2, rows, :], wu[lanes, :])
        ).astype(BF)
    backward = collect(backs.at[0], 1)
    backward.over_x()

    mid_across.wait_recv()
    spot = mid.at[:, pl.ds(pl.multiple_of(((me.dp + 2) % 4) * 128 + me.y * 32, 32), 32), :]
    mid_far = [send(spot, spot, sem_mid, 6 + k, me.at_y(k)) for k in range(1, me.tall)]
    for copy in mid_hidden:
        copy.wait_recv()
    for t in range(2):
        lanes = slice(t * 1024, (t + 1) * 1024)
        backs[1, :, lanes] = dot(mid[0, rows, :], wd[:, lanes]).astype(BF)
    backward.over_z()
    forward = collect(backs.at[1], 2)
    forward.over_x()
    spread_res.over_cores()
    spread_cot.over_cores()

    held = {}

    def pick_tall(k, slot, out):
        if slot == 1:
            order(turned, swap16, ordered, 16, 16, 2, k)
        if slot not in held:
            ids, count = ((gids, gcount), (uids, ucount))[slot - 1]
            held[slot] = own_hot(ids, count, "tall", 448, 60, 60, me.dp)
        pick(ordered, mid.at[slot], held[slot], out, flat, 16, 2, k)

    def pick_wide(k):
        if k == 0:
            turn(mid.at[0], turned, 0, 7)
            held[0] = own_hot(dids, dcount, "wide", 512, 60, 60, me.dp)
        order(turned, swap16, ordered, 16, 14, 1, k)
        pick(ordered, cot, held[0], od, flat, 16, 1, k)

    for k in range(4):
        work.append(lambda k=k: pick_tall(k, 1, og))
        work.append(lambda k=k: pick_tall(k, 2, ou))
    for k in range(4):
        work.append(lambda k=k: pick_wide(k))

    for copy in mid_far:
        copy.wait_recv()
    mid_cores = []
    for k, dp in enumerate((me.dp, (me.dp + 2) % 4)):
        spot = mid.at[:, pl.ds(pl.multiple_of(dp * 128, 128), 128), :]
        mid_cores.append(send(spot, spot, sem_mid, 10 + k, me.sibling()))
    spread_res.finish()
    turn(res, turned, 0, 16)

    total = edge[1] + backward.total()
    spread_ig = Spread(me, ig, sem_ig)
    spread_ig.over_z(total.astype(BF))
    swap_ig = swap_out(me, total, swap_from.at[0], swap_to.at[0], sem_swap, 1)
    for copy in mid_cores:
        copy.wait_recv()
    spread_cot.finish()
    fill(1)
    spread_ig.over_x(fill)
    forward.over_z()
    fill(1)

    rows = spread_ig.group()
    near_sums[me.y] = dot_nt(ig[rows, :], wh[...]).astype(BF)
    spot = near_sums.at[me.y]
    cg_copies = [send(spot, spot, sem_cg, k - 1, me.at_y(k)) for k in range(1, me.tall)]
    spread_ig.forward()
    fill(2)
    spread_ig.over_cores()

    total = residual.astype(BF).astype(F32) + forward.total()
    swap_layer = swap_out(me, total, swap_from.at[1], swap_to.at[1], sem_swap, 2)
    ctx_copies[1].wait_recv()
    spot = ctx.at[pl.ds(pl.multiple_of(((me.dp + 2) % 4) * 128, 128), 128), :]
    ctx_copies.append(send(spot, spot, sem_ctx, 2, me.sibling()))
    fill(len(work))
    swap_ig.wait_recv()
    input_grad[...] = swap_to[0].astype(BF)

    for copy in cg_copies:
        copy.wait_recv()
    total = near_sums[0].astype(F32)
    for k in range(1, me.tall):
        total = total + near_sums[k].astype(F32)
    context_grad[...] = total.astype(BF)
    swap_layer.wait_recv()
    layer[...] = swap_to[1].astype(BF)

    spread_ig.finish()
    for copy in [ctx_copies[0], ctx_copies[2]]:
        copy.wait_recv()
    for part in (spread_cot, spread_res, spread_ig, attention, backward, forward):
        part.drain()
    late = [entry, swap_ig, swap_layer, mid_across]
    late += ctx_copies + mid_deltas + mid_hidden + mid_far + mid_cores + cg_copies
    for slot in range(3):
        late += sum_copies[slot]
    for copy in late:
        copy.wait_send()


def chain_call(x8, cot8, context, lists, gate, up, down, heads):
    def sds(*shape):
        return jax.ShapeDtypeStruct(shape, BF)

    shapes = [
        sds(8, 2048), sds(8, 2048), sds(128, 256),
        sds(60, CELL), sds(60, CELL), sds(60, CELL), sds(512, 2048), sds(512, 256),
    ]
    dma = pltpu.SemaphoreType.DMA
    tall = lax.axis_size("in")
    depth = lax.axis_size("out") // 2
    return pl.pallas_call(
        chain_kernel,
        out_shape=shapes,
        in_specs=[VM] * 11 + [ANY] * 3 + [VM],
        out_specs=[VM] * 8,
        scratch_shapes=[
            pltpu.VMEM((512, 2048), BF),
            pltpu.VMEM((512, 2048), BF),
            pltpu.VMEM((3, 512, 896), BF),
            pltpu.VMEM((2048, 512), BF),
            pltpu.VMEM((512, 512), BF),
            pltpu.VMEM((512, 1024), BF),
            pltpu.VMEM((240, CELL), BF),
            pltpu.VMEM((240, CELL), BF),
            pltpu.VMEM((240, CELL), BF),
            pltpu.VMEM((512, 2048), BF),
            pltpu.VMEM((2048, 896), BF),
            pltpu.VMEM((2048, 896), BF),
            pltpu.VMEM((896, 2048), BF),
            pltpu.VMEM((256, 2048), BF),
            pltpu.VMEM((128, 2048), BF),
            pltpu.VMEM((2, 8, 2048), F32),
            pltpu.VMEM((2, 16, 1024), F32),
            pltpu.VMEM((3, 128, 1024), BF),
            pltpu.VMEM((3, 128, 1024), BF),
            pltpu.VMEM((3, depth - 1, 16, 1024), BF),
            pltpu.VMEM((2, 128, 2048), BF),
            pltpu.VMEM((3, 128, 896), F32),
            pltpu.VMEM((3, 128, 896), BF),
            pltpu.VMEM((tall - 1, 3, 32, 896), BF),
            pltpu.VMEM((2, 16, 1024), F32),
            pltpu.VMEM((2, 8, 2048), F32),
            pltpu.VMEM((tall, 128, 256), BF),
            dma((3,)),
            dma((2, 21)),
            dma((2, 21)),
            dma((2, 21)),
            dma((3, 2, 16)),
            dma((2, 3)),
            dma((3, 2, 3)),
            dma((2, 12)),
            dma((2, 3)),
            dma((2, 3)),
        ],
        compiler_params=pltpu.CompilerParams(
            collective_id=0, has_side_effects=True, vmem_limit_bytes=58 * 2**20
        ),
        name="chain",
    )(x8, cot8, context, *lists, gate, up, down, heads)


def local(
    inputs, context,
    gate_blocks, gate_ids, gate_count,
    up_blocks, up_ids, up_count,
    down_blocks, down_ids, down_count,
    heads_blocks, heads_ids, heads_count,
    cotangent,
):
    rows = lambda blocks: blocks.reshape(-1, CELL)
    line = lambda ids: ids.reshape(1, -1)
    lists = (
        line(gate_ids), gate_count, line(up_ids), up_count,
        line(down_ids), down_count, line(heads_ids), heads_count,
    )
    *results, ig, ctx = chain_call(
        inputs, cotangent, context, lists,
        rows(gate_blocks), rows(up_blocks), rows(down_blocks), rows(heads_blocks),
    )
    *done, og, ou, od, oh = finish_call(line(heads_ids), heads_count, ctx, ig, *results)
    return (*done, *(g.reshape(1, 1, -1, CELL) for g in (og, ou, od, oh)))


def solution(mesh):
    rows = P(("dp", "out"), "in")
    tall, wide = ("in", "out"), ("out", "in")

    def lists(axes):
        return P(*axes, None, None), P(*axes, None), P(*axes)

    return jax.shard_map(
        local,
        mesh=mesh,
        in_specs=(rows, P("dp", "out"), *lists(tall), *lists(tall), *lists(wide), *lists(wide), rows),
        out_specs=(
            rows,
            rows,
            P("dp", "out"),
            P(*tall, "dp", None),
            P(*tall, "dp", None),
            P(*wide, "dp", None),
            P(*wide, "dp", None),
        ),
        check_vma=False,
    )
```

```python
import jax
import jax.numpy as jnp
from jax import lax
from jax.experimental import pallas as pl
from jax.experimental.pallas import tpu as pltpu
from jax.sharding import PartitionSpec as P

BLOCK = 64
CELL = BLOCK * BLOCK
BF = jnp.bfloat16
F32 = jnp.float32
MESH = pl.DeviceIdType.MESH
VM = pl.BlockSpec(memory_space=pltpu.VMEM)
ANY = pl.BlockSpec(memory_space=pl.ANY)


def dot(a, b):
    return lax.dot_general(a, b, (((1,), (0,)), ((), ())), preferred_element_type=F32)


def dot_nt(a, b):
    return lax.dot_general(a, b, (((1,), (1,)), ((), ())), preferred_element_type=F32)


def dot_tn(a, b):
    return lax.dot_general(a, b, (((0,), (0,)), ((), ())), preferred_element_type=F32)


def one_hot(row, positions):
    spots = lax.broadcasted_iota(jnp.int32, (positions, row.shape[1]), 0)
    return jnp.where(spots == row, 1.0, 0.0).astype(BF)


def swap_matrix(inner, outer):
    rows = lax.broadcasted_iota(jnp.int32, (inner * outer, inner * outer), 0)
    cols = lax.broadcasted_iota(jnp.int32, (inner * outer, inner * outer), 1)
    source = (rows % outer) * inner + rows // outer
    return jnp.where(cols == source, 1.0, 0.0).astype(BF)


def halves(first, second):
    low = lax.broadcasted_iota(jnp.int32, first.shape, 1) < BLOCK
    return (
        jnp.where(low, first, pltpu.roll(second, BLOCK, 1)),
        jnp.where(low, pltpu.roll(first, BLOCK, 1), second),
    )


def spots(ids, count, kind):
    i = ids[...]
    if kind == "tall":
        r = (i * 2341) >> 15
        c = i - 14 * r
        spot = (r >> 4) * 224 + c * 16 + (r & 15)
    elif kind == "wide":
        spot = (i & 31) * 16 + (i >> 5)
    else:
        spot = (i & 31) * 8 + (i >> 5)
    slots = lax.broadcasted_iota(jnp.int32, i.shape, 1)
    return jnp.where(slots < count[...], spot, -1)


def place(hot, swap, blocks, stage, out, inner, used, stripes, k):
    chunk = 256 // inner
    width = out.shape[1]
    per = (width // BLOCK) * inner
    flat = dot(hot, blocks[:, k * chunk * BLOCK:(k + 1) * chunk * BLOCK]).astype(BF)
    for s in range(stripes):
        for p in range(chunk // 2):
            for q in range(width // 128):
                at = s * per + 2 * q * inner
                left = flat[at:at + inner, p * 128:(p + 1) * 128]
                right = flat[at + inner:at + 2 * inner, p * 128:(p + 1) * 128]
                pair = jnp.concatenate(halves(left, right), axis=0)
                at = s * 256 + 2 * p * inner
                stage[at:at + 2 * inner, q * 128:(q + 1) * 128] = pair
        dense = dot(swap, stage[s * 256:(s + 1) * 256, :width]).astype(BF)
        for r in range(used):
            at = s * inner * BLOCK + r * BLOCK + k * chunk
            out[at:at + chunk, :] = dense[r * chunk:(r + 1) * chunk]


def turn(left, turned, start, stop):
    for s in range(start, stop):
        turned[s * 128:(s + 1) * 128, :] = left[:, s * 128:(s + 1) * 128].T


def order(turned, swap, ordered, inner, used, stripes, k):
    chunk = 256 // inner
    for s in range(stripes):
        rows = [
            turned[s * used * BLOCK + r * BLOCK + k * chunk:s * used * BLOCK + r * BLOCK + (k + 1) * chunk, :]
            for r in range(used)
        ]
        rows += [jnp.zeros_like(rows[0])] * (inner - used)
        ordered[s * 256:(s + 1) * 256, :] = dot(swap, jnp.concatenate(rows, axis=0)).astype(BF)


def pick(ordered, right, hot, out, flat, inner, stripes, k):
    chunk = 256 // inner
    width = right.shape[1]
    piece = 1024 if width % 1024 == 0 else width
    for s in range(stripes):
        base = s * (width // BLOCK) * inner
        for t in range(width // piece):
            grad = dot(ordered[s * 256:(s + 1) * 256, :], right[:, t * piece:(t + 1) * piece]).astype(BF)
            for q in range(piece // 128):
                for p in range(chunk // 2):
                    pair = grad[2 * p * inner:(2 * p + 2) * inner, q * 128:(q + 1) * 128]
                    both = jnp.concatenate(halves(pair[:inner], pair[inner:]), axis=0)
                    at = base + (t * piece // 128 + q) * 2 * inner
                    flat[at:at + 2 * inner, p * 128:(p + 1) * 128] = both
    picked = dot_tn(hot, flat[:hot.shape[0], :chunk * BLOCK])
    out[:, k * chunk * BLOCK:(k + 1) * chunk * BLOCK] = picked.astype(BF)


def own_hot(ids, count, kind, positions, share, slots, dp):
    spot = spots(ids, count, kind)
    if slots > share:
        spot = jnp.concatenate([spot, jnp.full((1, slots - share), -1, jnp.int32)], axis=1)
    own = spot[:, :slots]
    for k in range(1, 4):
        own = jnp.where(dp == k, spot[:, k * share:k * share + slots], own)
    lanes = lax.broadcasted_iota(jnp.int32, own.shape, 1)
    return one_hot(jnp.where(lanes < share, own, -1), positions)


def finish_kernel(*refs):
    count = (len(refs) - 1) // 2
    copies = [pltpu.make_async_copy(refs[k], refs[count + k], refs[-1].at[k]) for k in range(count)]
    for copy in copies:
        copy.start()
    for copy in copies:
        copy.wait()


def finish_call(*results):
    return pl.pallas_call(
        finish_kernel,
        out_shape=[jax.ShapeDtypeStruct(r.shape, BF) for r in results],
        in_specs=[VM] * len(results),
        out_specs=[ANY] * len(results),
        scratch_shapes=[pltpu.SemaphoreType.DMA((len(results),))],
        compiler_params=pltpu.CompilerParams(vmem_limit_bytes=16 * 2**20),
        name="finish",
    )(*results)


class Links:

    def __init__(self):
        self.dp, self.y, self.out = lax.axis_index("dp"), lax.axis_index("in"), lax.axis_index("out")
        self.depth = lax.axis_size("out") // 2
        self.tall = lax.axis_size("in")
        self.core, self.z = self.dp % 2, self.out // 2
        self.low = self.out % 2
        self.x = (self.dp // 2) * 2 + self.low

    def at_x(self, k):
        x = (self.x + k) % 4
        return (x // 2) * 2 + self.core, self.y, self.z * 2 + x % 2

    def at_z(self, k):
        return self.dp, self.y, ((self.z + k) % self.depth) * 2 + self.low

    def at_y(self, k):
        return self.dp, (self.y + k) % self.tall, self.out

    def sibling(self):
        return (self.dp // 2) * 2 + 1 - self.core, self.y, self.out

    def beside(self):
        return self.dp, self.y, self.z * 2 + 1 - self.low

    def across(self):
        return (self.dp + 2) % 4, self.y, self.out

    def greet(self):
        barrier = pltpu.get_barrier_semaphore()
        peers = [self.at_x(k) for k in (1, 2, 3)]
        peers += [self.at_z(k) for k in range(1, self.depth)]
        peers += [self.at_y(k) for k in range(1, self.tall)]
        peers += [self.sibling()]
        for peer in peers:
            pl.semaphore_signal(barrier, inc=1, device_id=peer, device_id_type=MESH)
        return barrier, len(peers)

    def meet(self, greeted):
        pl.semaphore_wait(*greeted)


def send(source, target, sems, k, to):
    copy = pltpu.make_async_remote_copy(
        src_ref=source,
        dst_ref=target,
        send_sem=sems.at[0, k],
        recv_sem=sems.at[1, k],
        device_id=to,
        device_id_type=MESH,
    )
    copy.start()
    return copy


class Spread:

    def __init__(self, me, whole, sems, splits=1):
        self.me, self.whole, self.sems, self.width = me, whole, sems, 1024 // splits
        self.home = pl.ds(pl.multiple_of(me.low * 1024, 1024), 1024)
        self.away = pl.ds(pl.multiple_of((1 - me.low) * 1024, 1024), 1024)
        self.other = (me.dp + 2) % 4
        self.far = me.at_x(jnp.where(me.low == 0, 3, 1))
        self.sent, self.first, self.near = [], {}, []

    def rows(self, dp, start=0, size=128):
        return pl.ds(pl.multiple_of(dp * 128 + start, 16), size)

    def move(self, rows, lanes, k, to):
        spot = self.whole.at[rows, lanes]
        copy = send(spot, spot, self.sems, k, to)
        self.sent.append(copy)
        return copy

    def chunk(self, z):
        return pl.ds(pl.multiple_of(self.me.dp * 128 + (z % self.me.depth) * 16, 16), 16)

    def part(self, h):
        return pl.ds(pl.multiple_of(self.me.low * 1024 + h * self.width, self.width), self.width)

    def over_z(self, own, h=0):
        me = self.me
        self.whole[self.chunk(me.z), self.part(h)] = own
        ks = sorted(range(1, me.depth), key=lambda k: -min(k, me.depth - k))
        self.first[h] = {
            k: self.move(self.chunk(me.z), self.part(h), h * 8 + k, me.at_z(k)) for k in ks
        }

    def over_x(self, between=None, h=0):
        me, depth = self.me, self.me.depth
        at = 16 + h * 8
        self.near.append(self.move(self.chunk(me.z), self.part(h), at, me.beside()))
        for k in sorted(range(1, depth), key=lambda k: min(k, depth - k)):
            if between is not None and k < depth - k + 1:
                between(1)
            self.first[h][k].wait_recv()
            self.near.append(self.move(self.chunk(me.z + depth - k), self.part(h), at + k, me.beside()))

    def widen(self):
        self.wide = self.move(self.rows(self.me.dp), self.home, 32, self.far)

    def group(self):
        for copy in self.near:
            copy.wait_recv()
        return self.rows(self.me.dp)

    def forward(self):
        me = self.me
        self.half_a = self.move(self.rows(me.dp, 0, 64), self.away, 33, self.far)
        self.cores = [self.move(self.rows(me.dp), slice(None), 35, me.sibling())]
        self.wide.wait_recv()
        self.half_b = self.move(self.rows(self.other, 64, 64), self.away, 34, me.beside())

    def over_cores(self):
        self.half_a.wait_recv()
        self.half_b.wait_recv()
        self.cores.append(self.move(self.rows(self.other), slice(None), 36, self.me.sibling()))

    def finish(self):
        for copy in self.cores:
            copy.wait_recv()

    def drain(self):
        for copy in self.sent:
            copy.wait_send()


class Collect:

    def __init__(self, me, term, half, sums, parts, sems, splits=1):
        self.me, self.term, self.half, self.sums, self.parts, self.sems = me, term, half, sums, parts, sems
        self.width = 1024 // splits
        self.order = sorted(range(me.depth), key=lambda k: -min(k, me.depth - k))
        self.near, self.far, self.own = {}, {}, {}

    def chunk(self, k):
        return pl.ds(pl.multiple_of(((self.me.z + k) % self.me.depth) * 16, 16), 16)

    def lanes(self, h, low=0):
        return pl.ds(pl.multiple_of(low * 1024 + h * self.width, self.width), self.width)

    def over_x(self, h=0):
        for k in self.order:
            rows = self.chunk(k)
            self.near[h, k] = send(
                self.term.at[rows, self.lanes(h, 1 - self.me.low)], self.half.at[rows, self.lanes(h)],
                self.sems, h * 8 + k, self.me.beside(),
            )

    def over_z(self, h=0):
        me, lanes = self.me, self.lanes(h)
        for k in self.order:
            rows = self.chunk(k)
            self.near[h, k].wait_recv()
            both = self.term[rows, self.lanes(h, me.low)].astype(F32) + self.half[rows, lanes].astype(F32)
            if k == 0:
                self.own[h] = both
            else:
                self.sums[rows, lanes] = both.astype(BF)
                self.far[h, k] = send(
                    self.sums.at[rows, lanes], self.parts.at[k - 1, :, lanes], self.sems, 16 + h * 8 + k, me.at_z(k)
                )

    def total(self, h=0):
        total = self.own[h]
        for k in reversed(self.order[:-1]):
            self.far[h, k].wait_recv()
            total = total + self.parts[k - 1, :, self.lanes(h)].astype(F32)
        return total

    def drain(self):
        for copy in list(self.near.values()) + list(self.far.values()):
            copy.wait_send()


def swap_out(me, outgoing, landing, sems, k):
    away = outgoing.at[pl.ds(pl.multiple_of((1 - me.low) * 8, 8), 8), :]
    lanes = pl.ds(pl.multiple_of(me.low * 1024, 1024), 1024)
    landing[:, lanes] = outgoing[pl.ds(pl.multiple_of(me.low * 8, 8), 8), :]
    return send(away, landing.at[:, lanes], sems, k, me.beside())


def chain_kernel(
    x8, cot8, context, gids, gcount, uids, ucount, dids, dcount, hids, hcount, gate, up, down, heads,
    layer, input_grad, context_grad, og, ou, od, oh,
    ig, ctx, res, cot, mid, turned, ordered, flat, gate_in, up_in, down_in, stage, wg, wu, wd, wh, term,
    cells, edge, halves_in, sums, parts, backs,
    shares, shares_bf, gathered, swap_from, swap_to, near_sums,
    sem_in, sem_res, sem_cot, sem_ig, sem_rs, sem_ctx, sem_sum, sem_mid, sem_cg, sem_swap,
):
    loads = []
    for k, (source, target) in enumerate(((gate, gate_in), (up, up_in), (down, down_in))):
        loads.append(pltpu.make_async_copy(source, target, sem_in.at[k]))
        loads[-1].start()
    me = Links()
    greeted = me.greet()
    hot = one_hot(spots(hids, hcount, "heads"), 256)
    swap = swap_matrix(8, 32)
    for k in range(2):
        place(hot, swap, heads, stage, wh, 8, 4, 1, k)
    for t in range(2):
        cols = slice(t * 1024, (t + 1) * 1024)
        term[:, cols] = dot(context[...], wh[:, cols]).astype(BF)

    swap16 = swap_matrix(16, 16)
    work = []

    def queue(load, ids, count, kind, blocks, out, stripes, used):
        held = {}

        def step(k):
            if k == 0:
                loads[load].wait()
                held["hot"] = one_hot(spots(ids, count, kind), 448 if kind == "tall" else 512)
            place(held["hot"], swap16, blocks, stage, out, 16, used, stripes, k)

        for k in range(4):
            work.append(lambda k=k: step(k))

    queue(0, gids, gcount, "tall", gate_in, wg, 2, 16)
    queue(1, uids, ucount, "tall", up_in, wu, 2, 16)
    queue(2, dids, dcount, "wide", down_in, wd, 1, 14)

    def fill(n):
        for _ in range(n):
            work.pop(0)()

    low8 = pl.ds(pl.multiple_of(me.low * 8, 8), 8)
    away = pl.ds(pl.multiple_of((1 - me.low) * 1024, 1024), 1024)
    home = pl.ds(pl.multiple_of(me.low * 1024, 1024), 1024)

    def collect(term, k):
        return Collect(me, term, halves_in.at[k], sums.at[k], parts.at[k], sem_rs.at[k], 1 if k == 2 else 2)

    cells[0] = x8[...].astype(F32)
    cells[1] = cot8[...].astype(F32)
    edge[:, low8, :] = cells[:, :, home]
    me.meet(greeted)
    attention = collect(term, 0)
    attention.over_x(0)
    entry = send(cells.at[:, :, away], edge.at[:, low8, :], sem_swap, 0, me.beside())
    attention.over_x(1)
    fill(2)
    attention.over_z(0)
    fill(1)
    attention.over_z(1)
    entry.wait_recv()
    spread_cot = Spread(me, cot, sem_cot)
    spread_cot.over_z(edge[1].astype(BF))
    own_ctx = pl.ds(pl.multiple_of(me.dp * 128, 128), 128)
    ctx[own_ctx, :] = context[...]
    spot = ctx.at[own_ctx, :]
    ctx_copies = [send(spot, spot, sem_ctx, k, to) for k, to in enumerate((me.sibling(), me.across()))]
    fill(2)
    spread_res = Spread(me, res, sem_res, 2)
    for h in range(2):
        cols = slice(h * 512, (h + 1) * 512)
        spread_res.over_z((edge[0, :, cols] + attention.total(h)).astype(BF), h)
        fill(1)
    spread_cot.over_x()
    spread_cot.widen()
    fill(1)
    spread_res.over_x(None, 0)
    fill(1)
    spread_res.over_x(None, 1)
    spread_res.widen()
    fill(3)

    def share(slot):
        copies = []
        for k in range(1, me.tall):
            rows = pl.ds(pl.multiple_of(((me.y + k) % me.tall) * 32, 32), 32)
            copies.append(
                send(shares_bf.at[slot, rows, :], gathered.at[k - 1, slot], sem_sum.at[slot], k - 1, me.at_y(k))
            )
        return copies

    rows = spread_cot.group()
    for t in range(2):
        lanes = slice(t * 512, min(896, (t + 1) * 512))
        shares[2, :, lanes] = dot_nt(cot[rows, :], wd[lanes, :])
    shares_bf[2] = shares[2].astype(BF)
    sum_copies = {2: share(2)}

    rows = spread_res.group()
    for slot, weight in ((0, wg), (1, wu)):
        shares[slot] = dot(res[rows, :], weight[...])
        shares_bf[slot] = shares[slot].astype(BF)
        sum_copies[slot] = share(slot)

    spread_cot.forward()
    quarter = pl.ds(pl.multiple_of(me.y * 32, 32), 32)

    def total_of(slot):
        total = shares[slot, quarter, :]
        for k in range(me.tall - 1):
            sum_copies[slot][k].wait_recv()
            total = total + gathered[k, slot].astype(F32)
        return total

    hidden_grad = total_of(2)
    gate_sum = total_of(0)
    sigmoid = 1.0 / (1.0 + jnp.exp(-gate_sum))
    slope = hidden_grad * sigmoid * (1.0 + gate_sum * (1.0 - sigmoid))
    swish = gate_sum * sigmoid
    up_sum = total_of(1)
    spot_rows = pl.ds(pl.multiple_of(me.dp * 128 + me.y * 32, 32), 32)
    mid[1, spot_rows, :] = (slope * up_sum).astype(BF)
    mid[2, spot_rows, :] = (hidden_grad * swish).astype(BF)
    spot = mid.at[pl.ds(1, 2), spot_rows, :]
    mid_deltas = [send(spot, spot, sem_mid, k - 1, me.at_y(k)) for k in range(1, me.tall)]
    mid[0, spot_rows, :] = (swish * up_sum).astype(BF)
    spot = mid.at[0, spot_rows, :]
    mid_hidden = [send(spot, spot, sem_mid, 2 + k, me.at_y(k)) for k in range(1, me.tall)]
    spot = mid.at[:, spot_rows, :]
    mid_across = send(spot, spot, sem_mid, 6, me.across())
    spread_res.forward()
    for copy in mid_deltas:
        copy.wait_recv()

    rows = pl.ds(pl.multiple_of(me.dp * 128, 128), 128)
    for t in range(4):
        lanes = slice(t * 512, (t + 1) * 512)
        backs[0, :, lanes] = (
            dot_nt(mid[1, rows, :], wg[lanes, :]) + dot_nt(mid[2, rows, :], wu[lanes, :])
        ).astype(BF)
    backward = collect(backs.at[0], 1)
    backward.over_x(0)
    backward.over_x(1)

    mid_across.wait_recv()
    spot = mid.at[:, pl.ds(pl.multiple_of(((me.dp + 2) % 4) * 128 + me.y * 32, 32), 32), :]
    mid_far = [send(spot, spot, sem_mid, 6 + k, me.at_y(k)) for k in range(1, me.tall)]
    for copy in mid_hidden:
        copy.wait_recv()
    for t in range(2):
        lanes = slice(t * 1024, (t + 1) * 1024)
        backs[1, :, lanes] = dot(mid[0, rows, :], wd[:, lanes]).astype(BF)
    backward.over_z(0)
    backward.over_z(1)
    forward = collect(backs.at[1], 2)
    forward.over_x()
    spread_res.over_cores()
    spread_cot.over_cores()

    held = {}

    def pick_tall(k, slot, out):
        if slot == 1:
            order(turned, swap16, ordered, 16, 16, 2, k)
        if slot not in held:
            ids, count = ((gids, gcount), (uids, ucount))[slot - 1]
            held[slot] = own_hot(ids, count, "tall", 448, 60, 60, me.dp)
        pick(ordered, mid.at[slot], held[slot], out, flat, 16, 2, k)

    def pick_wide(k):
        if k == 0:
            turn(mid.at[0], turned, 0, 7)
            held[0] = own_hot(dids, dcount, "wide", 512, 60, 60, me.dp)
        order(turned, swap16, ordered, 16, 14, 1, k)
        pick(ordered, cot, held[0], od, flat, 16, 1, k)

    for k in range(4):
        work.append(lambda k=k: pick_tall(k, 1, og))
        work.append(lambda k=k: pick_tall(k, 2, ou))
    for k in range(4):
        work.append(lambda k=k: pick_wide(k))

    for copy in mid_far:
        copy.wait_recv()
    mid_cores = []
    for k, dp in enumerate((me.dp, (me.dp + 2) % 4)):
        spot = mid.at[:, pl.ds(pl.multiple_of(dp * 128, 128), 128), :]
        mid_cores.append(send(spot, spot, sem_mid, 10 + k, me.sibling()))
    spread_res.finish()
    turn(res, turned, 0, 16)

    spread_ig = Spread(me, ig, sem_ig, 2)
    for h in range(2):
        cols = slice(h * 512, (h + 1) * 512)
        total = edge[1, :, cols] + backward.total(h)
        spread_ig.over_z(total.astype(BF), h)
        swap_from[0, :, cols] = total
    swap_ig = swap_out(me, swap_from.at[0], swap_to.at[0], sem_swap, 1)
    for copy in mid_cores:
        copy.wait_recv()
    spread_cot.finish()
    fill(1)
    spread_ig.over_x(fill, 0)
    spread_ig.over_x(None, 1)
    spread_ig.widen()
    forward.over_z()
    fill(1)

    rows = spread_ig.group()
    near_sums[me.y] = dot_nt(ig[rows, :], wh[...]).astype(BF)
    spot = near_sums.at[me.y]
    cg_copies = [send(spot, spot, sem_cg, k - 1, me.at_y(k)) for k in range(1, me.tall)]
    spread_ig.forward()
    fill(2)
    spread_ig.over_cores()

    swap_from[1] = res[spread_res.chunk(me.z), home].astype(F32) + forward.total()
    swap_layer = swap_out(me, swap_from.at[1], swap_to.at[1], sem_swap, 2)
    ctx_copies[1].wait_recv()
    spot = ctx.at[pl.ds(pl.multiple_of(((me.dp + 2) % 4) * 128, 128), 128), :]
    ctx_copies.append(send(spot, spot, sem_ctx, 2, me.sibling()))
    fill(len(work))
    swap_ig.wait_recv()
    input_grad[...] = swap_to[0].astype(BF)

    for copy in cg_copies:
        copy.wait_recv()
    total = near_sums[0].astype(F32)
    for k in range(1, me.tall):
        total = total + near_sums[k].astype(F32)
    context_grad[...] = total.astype(BF)
    swap_layer.wait_recv()
    layer[...] = swap_to[1].astype(BF)

    for copy in [ctx_copies[0], ctx_copies[2]]:
        copy.wait_recv()
    turn(ctx, turned, 0, 2)
    swap = swap_matrix(32, 8)
    hot = own_hot(hids, hcount, "heads", 256, 17, 17, me.dp)
    for k in range(2):
        order(turned, swap, ordered.at[pl.ds(k * 256, 256), :], 8, 4, 1, k)
    spread_ig.finish()
    for k in range(2):
        pick(ordered.at[pl.ds(k * 256, 256), :], ig, hot, oh, flat, 8, 1, k)
    for part in (spread_cot, spread_res, spread_ig, attention, backward, forward):
        part.drain()
    late = [entry, swap_ig, swap_layer, mid_across]
    late += ctx_copies + mid_deltas + mid_hidden + mid_far + mid_cores + cg_copies
    for slot in range(3):
        late += sum_copies[slot]
    for copy in late:
        copy.wait_send()


def chain_call(x8, cot8, context, lists, gate, up, down, heads):
    def sds(*shape):
        return jax.ShapeDtypeStruct(shape, BF)

    shapes = [
        sds(8, 2048), sds(8, 2048), sds(128, 256),
        sds(60, CELL), sds(60, CELL), sds(60, CELL), sds(17, CELL),
    ]
    dma = pltpu.SemaphoreType.DMA
    tall = lax.axis_size("in")
    depth = lax.axis_size("out") // 2
    return pl.pallas_call(
        chain_kernel,
        out_shape=shapes,
        in_specs=[VM] * 11 + [ANY] * 3 + [VM],
        out_specs=[VM] * 7,
        scratch_shapes=[
            pltpu.VMEM((512, 2048), BF),
            pltpu.VMEM((512, 256), BF),
            pltpu.VMEM((512, 2048), BF),
            pltpu.VMEM((512, 2048), BF),
            pltpu.VMEM((3, 512, 896), BF),
            pltpu.VMEM((2048, 512), BF),
            pltpu.VMEM((512, 512), BF),
            pltpu.VMEM((512, 2048), BF),
            pltpu.VMEM((240, CELL), BF),
            pltpu.VMEM((240, CELL), BF),
            pltpu.VMEM((240, CELL), BF),
            pltpu.VMEM((512, 2048), BF),
            pltpu.VMEM((2048, 896), BF),
            pltpu.VMEM((2048, 896), BF),
            pltpu.VMEM((896, 2048), BF),
            pltpu.VMEM((256, 2048), BF),
            pltpu.VMEM((128, 2048), BF),
            pltpu.VMEM((2, 8, 2048), F32),
            pltpu.VMEM((2, 16, 1024), F32),
            pltpu.VMEM((3, 128, 1024), BF),
            pltpu.VMEM((3, 128, 1024), BF),
            pltpu.VMEM((3, depth - 1, 16, 1024), BF),
            pltpu.VMEM((2, 128, 2048), BF),
            pltpu.VMEM((3, 128, 896), F32),
            pltpu.VMEM((3, 128, 896), BF),
            pltpu.VMEM((tall - 1, 3, 32, 896), BF),
            pltpu.VMEM((2, 16, 1024), F32),
            pltpu.VMEM((2, 8, 2048), F32),
            pltpu.VMEM((tall, 128, 256), BF),
            dma((3,)),
            dma((2, 37)),
            dma((2, 37)),
            dma((2, 37)),
            dma((3, 2, 32)),
            dma((2, 3)),
            dma((3, 2, 3)),
            dma((2, 12)),
            dma((2, 3)),
            dma((2, 3)),
        ],
        compiler_params=pltpu.CompilerParams(
            collective_id=0, has_side_effects=True, vmem_limit_bytes=58 * 2**20
        ),
        name="chain",
    )(x8, cot8, context, *lists, gate, up, down, heads)


def local(
    inputs, context,
    gate_blocks, gate_ids, gate_count,
    up_blocks, up_ids, up_count,
    down_blocks, down_ids, down_count,
    heads_blocks, heads_ids, heads_count,
    cotangent,
):
    rows = lambda blocks: blocks.reshape(-1, CELL)
    line = lambda ids: ids.reshape(1, -1)
    lists = (
        line(gate_ids), gate_count, line(up_ids), up_count,
        line(down_ids), down_count, line(heads_ids), heads_count,
    )
    results = chain_call(
        inputs, cotangent, context, lists,
        rows(gate_blocks), rows(up_blocks), rows(down_blocks), rows(heads_blocks),
    )
    done = finish_call(*results)
    return (*done[:3], *(g.reshape(1, 1, -1, CELL) for g in done[3:]))


def solution(mesh):
    rows = P(("dp", "out"), "in")
    tall, wide = ("in", "out"), ("out", "in")

    def lists(axes):
        return P(*axes, None, None), P(*axes, None), P(*axes)

    return jax.shard_map(
        local,
        mesh=mesh,
        in_specs=(rows, P("dp", "out"), *lists(tall), *lists(tall), *lists(wide), *lists(wide), rows),
        out_specs=(
            rows,
            rows,
            P("dp", "out"),
            P(*tall, "dp", None),
            P(*tall, "dp", None),
            P(*wide, "dp", None),
            P(*wide, "dp", None),
        ),
        check_vma=False,
    )
```

```python
import jax
import jax.numpy as jnp
from jax import lax
from jax.experimental import pallas as pl
from jax.experimental.pallas import tpu as pltpu
from jax.sharding import PartitionSpec as P

BLOCK = 64
CELL = BLOCK * BLOCK
BF = jnp.bfloat16
F32 = jnp.float32
MESH = pl.DeviceIdType.MESH
VM = pl.BlockSpec(memory_space=pltpu.VMEM)
ANY = pl.BlockSpec(memory_space=pl.ANY)


def dot(a, b):
    return lax.dot_general(a, b, (((1,), (0,)), ((), ())), preferred_element_type=F32)


def dot_nt(a, b):
    return lax.dot_general(a, b, (((1,), (1,)), ((), ())), preferred_element_type=F32)


def dot_tn(a, b):
    return lax.dot_general(a, b, (((0,), (0,)), ((), ())), preferred_element_type=F32)


def one_hot(row, positions):
    spots = lax.broadcasted_iota(jnp.int32, (positions, row.shape[1]), 0)
    return jnp.where(spots == row, 1.0, 0.0).astype(BF)


def swap_matrix(inner, outer):
    rows = lax.broadcasted_iota(jnp.int32, (inner * outer, inner * outer), 0)
    cols = lax.broadcasted_iota(jnp.int32, (inner * outer, inner * outer), 1)
    source = (rows % outer) * inner + rows // outer
    return jnp.where(cols == source, 1.0, 0.0).astype(BF)


def halves(first, second):
    low = lax.broadcasted_iota(jnp.int32, first.shape, 1) < BLOCK
    return (
        jnp.where(low, first, pltpu.roll(second, BLOCK, 1)),
        jnp.where(low, pltpu.roll(first, BLOCK, 1), second),
    )


def spots(ids, count, kind):
    i = ids[...]
    if kind == "tall":
        r = (i * 2341) >> 15
        c = i - 14 * r
        spot = (r >> 4) * 224 + c * 16 + (r & 15)
    elif kind == "wide":
        spot = (i & 31) * 16 + (i >> 5)
    else:
        spot = (i & 31) * 8 + (i >> 5)
    slots = lax.broadcasted_iota(jnp.int32, i.shape, 1)
    return jnp.where(slots < count[...], spot, -1)


def place(hot, swap, blocks, stage, out, inner, used, stripes, k):
    chunk = 256 // inner
    width = out.shape[1]
    per = (width // BLOCK) * inner
    flat = dot(hot, blocks[:, k * chunk * BLOCK:(k + 1) * chunk * BLOCK]).astype(BF)
    for s in range(stripes):
        for p in range(chunk // 2):
            for q in range(width // 128):
                at = s * per + 2 * q * inner
                left = flat[at:at + inner, p * 128:(p + 1) * 128]
                right = flat[at + inner:at + 2 * inner, p * 128:(p + 1) * 128]
                pair = jnp.concatenate(halves(left, right), axis=0)
                at = s * 256 + 2 * p * inner
                stage[at:at + 2 * inner, q * 128:(q + 1) * 128] = pair
        dense = dot(swap, stage[s * 256:(s + 1) * 256, :width]).astype(BF)
        for r in range(used):
            at = s * inner * BLOCK + r * BLOCK + k * chunk
            out[at:at + chunk, :] = dense[r * chunk:(r + 1) * chunk]


def turn(left, turned, start, stop):
    for s in range(start, stop):
        turned[s * 128:(s + 1) * 128, :] = left[:, s * 128:(s + 1) * 128].T


def order(turned, swap, ordered, inner, used, stripes, k):
    chunk = 256 // inner
    for s in range(stripes):
        rows = [
            turned[s * used * BLOCK + r * BLOCK + k * chunk:s * used * BLOCK + r * BLOCK + (k + 1) * chunk, :]
            for r in range(used)
        ]
        rows += [jnp.zeros_like(rows[0])] * (inner - used)
        ordered[s * 256:(s + 1) * 256, :] = dot(swap, jnp.concatenate(rows, axis=0)).astype(BF)


def pick(ordered, right, hot, out, flat, inner, stripes, k):
    chunk = 256 // inner
    width = right.shape[1]
    piece = 1024 if width % 1024 == 0 else width
    for s in range(stripes):
        base = s * (width // BLOCK) * inner
        for t in range(width // piece):
            grad = dot(ordered[s * 256:(s + 1) * 256, :], right[:, t * piece:(t + 1) * piece]).astype(BF)
            for q in range(piece // 128):
                for p in range(chunk // 2):
                    pair = grad[2 * p * inner:(2 * p + 2) * inner, q * 128:(q + 1) * 128]
                    both = jnp.concatenate(halves(pair[:inner], pair[inner:]), axis=0)
                    at = base + (t * piece // 128 + q) * 2 * inner
                    flat[at:at + 2 * inner, p * 128:(p + 1) * 128] = both
    picked = dot_tn(hot, flat[:hot.shape[0], :chunk * BLOCK])
    out[:, k * chunk * BLOCK:(k + 1) * chunk * BLOCK] = picked.astype(BF)


def own_hot(ids, count, kind, positions, share, slots, dp):
    spot = spots(ids, count, kind)
    if slots > share:
        spot = jnp.concatenate([spot, jnp.full((1, slots - share), -1, jnp.int32)], axis=1)
    own = spot[:, :slots]
    for k in range(1, 4):
        own = jnp.where(dp == k, spot[:, k * share:k * share + slots], own)
    lanes = lax.broadcasted_iota(jnp.int32, own.shape, 1)
    return one_hot(jnp.where(lanes < share, own, -1), positions)


def finish_kernel(*refs):
    count = (len(refs) - 1) // 3
    sources, targets, held, sems = refs[:count], refs[count:2 * count], refs[2 * count:-1], refs[-1]
    loads = [pltpu.make_async_copy(sources[k], held[k], sems.at[0, k]) for k in range(count)]
    stores = [pltpu.make_async_copy(held[k], targets[k], sems.at[1, k]) for k in range(count)]
    for copy in loads:
        copy.start()
    for load, store in zip(loads, stores):
        load.wait()
        store.start()
    for copy in stores:
        copy.wait()


def finish_call(*results):
    return pl.pallas_call(
        finish_kernel,
        out_shape=[jax.ShapeDtypeStruct(r.shape, BF) for r in results],
        in_specs=[ANY] * len(results),
        out_specs=[ANY] * len(results),
        scratch_shapes=[pltpu.VMEM(r.shape, BF) for r in results]
        + [pltpu.SemaphoreType.DMA((2, len(results)))],
        compiler_params=pltpu.CompilerParams(vmem_limit_bytes=58 * 2**20),
        name="finish",
    )(*results)


class Links:

    def __init__(self):
        self.dp, self.y, self.out = lax.axis_index("dp"), lax.axis_index("in"), lax.axis_index("out")
        self.depth = lax.axis_size("out") // 2
        self.tall = lax.axis_size("in")
        self.core, self.z = self.dp % 2, self.out // 2
        self.low = self.out % 2
        self.x = (self.dp // 2) * 2 + self.low

    def at_x(self, k):
        x = (self.x + k) % 4
        return (x // 2) * 2 + self.core, self.y, self.z * 2 + x % 2

    def at_z(self, k):
        return self.dp, self.y, ((self.z + k) % self.depth) * 2 + self.low

    def at_y(self, k):
        return self.dp, (self.y + k) % self.tall, self.out

    def sibling(self):
        return (self.dp // 2) * 2 + 1 - self.core, self.y, self.out

    def beside(self):
        return self.dp, self.y, self.z * 2 + 1 - self.low

    def across(self):
        return (self.dp + 2) % 4, self.y, self.out

    def greet(self):
        barrier = pltpu.get_barrier_semaphore()
        peers = [self.at_x(k) for k in (1, 2, 3)]
        peers += [self.at_z(k) for k in range(1, self.depth)]
        peers += [self.at_y(k) for k in range(1, self.tall)]
        peers += [self.sibling()]
        for peer in peers:
            pl.semaphore_signal(barrier, inc=1, device_id=peer, device_id_type=MESH)
        return barrier, len(peers)

    def meet(self, greeted):
        pl.semaphore_wait(*greeted)


def send(source, target, sems, k, to):
    copy = pltpu.make_async_remote_copy(
        src_ref=source,
        dst_ref=target,
        send_sem=sems.at[0, k],
        recv_sem=sems.at[1, k],
        device_id=to,
        device_id_type=MESH,
    )
    copy.start()
    return copy


class Spread:

    def __init__(self, me, whole, sems, splits=1):
        self.me, self.whole, self.sems, self.width = me, whole, sems, 1024 // splits
        self.home = pl.ds(pl.multiple_of(me.low * 1024, 1024), 1024)
        self.away = pl.ds(pl.multiple_of((1 - me.low) * 1024, 1024), 1024)
        self.other = (me.dp + 2) % 4
        self.far = me.at_x(jnp.where(me.low == 0, 3, 1))
        self.sent, self.first, self.near = [], {}, []

    def rows(self, dp, start=0, size=128):
        return pl.ds(pl.multiple_of(dp * 128 + start, 16), size)

    def move(self, rows, lanes, k, to):
        spot = self.whole.at[rows, lanes]
        copy = send(spot, spot, self.sems, k, to)
        self.sent.append(copy)
        return copy

    def chunk(self, z):
        return pl.ds(pl.multiple_of(self.me.dp * 128 + (z % self.me.depth) * 16, 16), 16)

    def part(self, h):
        return pl.ds(pl.multiple_of(self.me.low * 1024 + h * self.width, self.width), self.width)

    def over_z(self, own, h=0):
        me = self.me
        self.whole[self.chunk(me.z), self.part(h)] = own
        ks = sorted(range(1, me.depth), key=lambda k: -min(k, me.depth - k))
        self.first[h] = {
            k: self.move(self.chunk(me.z), self.part(h), h * 8 + k, me.at_z(k)) for k in ks
        }

    def over_x(self, between=None, h=0):
        me, depth = self.me, self.me.depth
        at = 16 + h * 8
        self.near.append(self.move(self.chunk(me.z), self.part(h), at, me.beside()))
        for k in sorted(range(1, depth), key=lambda k: min(k, depth - k)):
            if between is not None and k < depth - k + 1:
                between(1)
            self.first[h][k].wait_recv()
            self.near.append(self.move(self.chunk(me.z + depth - k), self.part(h), at + k, me.beside()))

    def widen(self):
        self.wide = self.move(self.rows(self.me.dp), self.home, 32, self.far)

    def group(self):
        for copy in self.near:
            copy.wait_recv()
        return self.rows(self.me.dp)

    def forward(self):
        me = self.me
        self.half_a = self.move(self.rows(me.dp, 0, 64), self.away, 33, self.far)
        self.cores = [self.move(self.rows(me.dp), slice(None), 35, me.sibling())]
        self.wide.wait_recv()
        self.half_b = self.move(self.rows(self.other, 64, 64), self.away, 34, me.beside())

    def over_cores(self):
        self.half_a.wait_recv()
        self.half_b.wait_recv()
        self.cores.append(self.move(self.rows(self.other), slice(None), 36, self.me.sibling()))

    def finish(self):
        for copy in self.cores:
            copy.wait_recv()

    def drain(self):
        for copy in self.sent:
            copy.wait_send()


class Collect:

    def __init__(self, me, term, half, sums, parts, sems, splits=1):
        self.me, self.term, self.half, self.sums, self.parts, self.sems = me, term, half, sums, parts, sems
        self.width = 1024 // splits
        self.order = sorted(range(me.depth), key=lambda k: -min(k, me.depth - k))
        self.near, self.far, self.own = {}, {}, {}

    def chunk(self, k):
        return pl.ds(pl.multiple_of(((self.me.z + k) % self.me.depth) * 16, 16), 16)

    def lanes(self, h, low=0):
        return pl.ds(pl.multiple_of(low * 1024 + h * self.width, self.width), self.width)

    def over_x(self, h=0):
        for k in self.order:
            rows = self.chunk(k)
            self.near[h, k] = send(
                self.term.at[rows, self.lanes(h, 1 - self.me.low)], self.half.at[rows, self.lanes(h)],
                self.sems, h * 8 + k, self.me.beside(),
            )

    def over_z(self, h=0):
        me, lanes = self.me, self.lanes(h)
        for k in self.order:
            rows = self.chunk(k)
            self.near[h, k].wait_recv()
            both = self.term[rows, self.lanes(h, me.low)].astype(F32) + self.half[rows, lanes].astype(F32)
            if k == 0:
                self.own[h] = both
            else:
                self.sums[rows, lanes] = both.astype(BF)
                self.far[h, k] = send(
                    self.sums.at[rows, lanes], self.parts.at[k - 1, :, lanes], self.sems, 16 + h * 8 + k, me.at_z(k)
                )

    def total(self, h=0):
        total = self.own[h]
        for k in reversed(self.order[:-1]):
            self.far[h, k].wait_recv()
            total = total + self.parts[k - 1, :, self.lanes(h)].astype(F32)
        return total

    def drain(self):
        for copy in list(self.near.values()) + list(self.far.values()):
            copy.wait_send()


def swap_out(me, outgoing, landing, sems, k):
    away = outgoing.at[pl.ds(pl.multiple_of((1 - me.low) * 8, 8), 8), :]
    lanes = pl.ds(pl.multiple_of(me.low * 1024, 1024), 1024)
    landing[:, lanes] = outgoing[pl.ds(pl.multiple_of(me.low * 8, 8), 8), :]
    return send(away, landing.at[:, lanes], sems, k, me.beside())


def chain_kernel(
    x8, cot8, context, gids, gcount, uids, ucount, dids, dcount, hids, hcount, gate, up, down, heads,
    layer, input_grad, context_grad, og, ou, od, oh,
    ig, ctx, res, cot, mid, turned, ordered, flat, gate_in, up_in, down_in, stage, wg, wu, wd, wh, term,
    cells, edge, halves_in, sums, parts, backs,
    shares, shares_bf, gathered, swap_from, swap_to, near_sums,
    sem_in, sem_res, sem_cot, sem_ig, sem_rs, sem_ctx, sem_sum, sem_mid, sem_cg, sem_swap,
):
    loads = []
    for k, (source, target) in enumerate(((gate, gate_in), (up, up_in), (down, down_in))):
        loads.append(pltpu.make_async_copy(source, target, sem_in.at[k]))
        loads[-1].start()
    me = Links()
    greeted = me.greet()
    hot = one_hot(spots(hids, hcount, "heads"), 256)
    swap = swap_matrix(8, 32)
    for k in range(2):
        place(hot, swap, heads, stage, wh, 8, 4, 1, k)
    for t in range(2):
        cols = slice(t * 1024, (t + 1) * 1024)
        term[:, cols] = dot(context[...], wh[:, cols]).astype(BF)

    swap16 = swap_matrix(16, 16)
    work = []

    def queue(load, ids, count, kind, blocks, out, stripes, used):
        held = {}

        def step(k):
            if k == 0:
                loads[load].wait()
                held["hot"] = one_hot(spots(ids, count, kind), 448 if kind == "tall" else 512)
            place(held["hot"], swap16, blocks, stage, out, 16, used, stripes, k)

        for k in range(4):
            work.append(lambda k=k: step(k))

    queue(0, gids, gcount, "tall", gate_in, wg, 2, 16)
    queue(1, uids, ucount, "tall", up_in, wu, 2, 16)
    queue(2, dids, dcount, "wide", down_in, wd, 1, 14)

    def fill(n):
        for _ in range(n):
            work.pop(0)()

    low8 = pl.ds(pl.multiple_of(me.low * 8, 8), 8)
    away = pl.ds(pl.multiple_of((1 - me.low) * 1024, 1024), 1024)
    home = pl.ds(pl.multiple_of(me.low * 1024, 1024), 1024)

    def collect(term, k):
        return Collect(me, term, halves_in.at[k], sums.at[k], parts.at[k], sem_rs.at[k], 1 if k == 2 else 2)

    cells[0] = x8[...].astype(F32)
    cells[1] = cot8[...].astype(F32)
    edge[:, low8, :] = cells[:, :, home]
    me.meet(greeted)
    attention = collect(term, 0)
    attention.over_x(0)
    entry = send(cells.at[:, :, away], edge.at[:, low8, :], sem_swap, 0, me.beside())
    attention.over_x(1)
    fill(2)
    attention.over_z(0)
    fill(1)
    attention.over_z(1)
    entry.wait_recv()
    spread_cot = Spread(me, cot, sem_cot)
    spread_cot.over_z(edge[1].astype(BF))
    own_ctx = pl.ds(pl.multiple_of(me.dp * 128, 128), 128)
    ctx[own_ctx, :] = context[...]
    spot = ctx.at[own_ctx, :]
    ctx_copies = [send(spot, spot, sem_ctx, k, to) for k, to in enumerate((me.sibling(), me.across()))]
    fill(2)
    spread_res = Spread(me, res, sem_res, 2)
    for h in range(2):
        cols = slice(h * 512, (h + 1) * 512)
        spread_res.over_z((edge[0, :, cols] + attention.total(h)).astype(BF), h)
        fill(1)
    spread_cot.over_x()
    spread_cot.widen()
    fill(1)
    spread_res.over_x(None, 0)
    fill(1)
    spread_res.over_x(None, 1)
    spread_res.widen()
    fill(3)

    def share(slot):
        copies = []
        for k in range(1, me.tall):
            rows = pl.ds(pl.multiple_of(((me.y + k) % me.tall) * 32, 32), 32)
            copies.append(
                send(shares_bf.at[slot, rows, :], gathered.at[k - 1, slot], sem_sum.at[slot], k - 1, me.at_y(k))
            )
        return copies

    rows = spread_cot.group()
    for t in range(2):
        lanes = slice(t * 512, min(896, (t + 1) * 512))
        shares[2, :, lanes] = dot_nt(cot[rows, :], wd[lanes, :])
    shares_bf[2] = shares[2].astype(BF)
    sum_copies = {2: share(2)}

    rows = spread_res.group()
    for slot, weight in ((0, wg), (1, wu)):
        shares[slot] = dot(res[rows, :], weight[...])
        shares_bf[slot] = shares[slot].astype(BF)
        sum_copies[slot] = share(slot)

    spread_cot.forward()
    spread_res.forward()
    quarter = pl.ds(pl.multiple_of(me.y * 32, 32), 32)

    def total_of(slot):
        total = shares[slot, quarter, :]
        for k in range(me.tall - 1):
            sum_copies[slot][k].wait_recv()
            total = total + gathered[k, slot].astype(F32)
        return total

    hidden_grad = total_of(2)
    gate_sum = total_of(0)
    sigmoid = 1.0 / (1.0 + jnp.exp(-gate_sum))
    slope = hidden_grad * sigmoid * (1.0 + gate_sum * (1.0 - sigmoid))
    swish = gate_sum * sigmoid
    up_sum = total_of(1)
    spot_rows = pl.ds(pl.multiple_of(me.dp * 128 + me.y * 32, 32), 32)
    mid[1, spot_rows, :] = (slope * up_sum).astype(BF)
    mid[2, spot_rows, :] = (hidden_grad * swish).astype(BF)
    spot = mid.at[pl.ds(1, 2), spot_rows, :]
    mid_deltas = [send(spot, spot, sem_mid, k - 1, me.at_y(k)) for k in range(1, me.tall)]
    mid[0, spot_rows, :] = (swish * up_sum).astype(BF)
    spot = mid.at[0, spot_rows, :]
    mid_hidden = [send(spot, spot, sem_mid, 2 + k, me.at_y(k)) for k in range(1, me.tall)]
    spot = mid.at[:, spot_rows, :]
    mid_across = send(spot, spot, sem_mid, 6, me.across())
    spread_res.over_cores()
    spread_cot.over_cores()
    spread_res.finish()
    turn(res, turned, 0, 16)
    for copy in mid_deltas:
        copy.wait_recv()

    mid_across.wait_recv()
    spot = mid.at[:, pl.ds(pl.multiple_of(((me.dp + 2) % 4) * 128 + me.y * 32, 32), 32), :]
    mid_far = [send(spot, spot, sem_mid, 6 + k, me.at_y(k)) for k in range(1, me.tall)]

    rows = pl.ds(pl.multiple_of(me.dp * 128, 128), 128)
    backward = collect(backs.at[0], 1)
    for low in (1 - me.low, me.low):
        for h in range(2):
            lanes = pl.ds(pl.multiple_of(low * 1024 + h * 512, 512), 512)
            backs[0, :, lanes] = (
                dot_nt(mid[1, rows, :], wg[lanes, :]) + dot_nt(mid[2, rows, :], wu[lanes, :])
            ).astype(BF)
            if low is not me.low:
                backward.over_x(h)
    backward.over_z(0)
    backward.over_z(1)
    for copy in mid_hidden:
        copy.wait_recv()
    spot = mid.at[:, rows, :]
    mid_cores = [send(spot, spot, sem_mid, 10, me.sibling())]
    for t in range(2):
        lanes = slice(t * 1024, (t + 1) * 1024)
        backs[1, :, lanes] = dot(mid[0, rows, :], wd[:, lanes]).astype(BF)
    forward = collect(backs.at[1], 2)
    forward.over_x()

    held = {}

    def pick_tall(k, slot, out):
        if slot == 1:
            order(turned, swap16, ordered, 16, 16, 2, k)
        if slot not in held:
            ids, count = ((gids, gcount), (uids, ucount))[slot - 1]
            held[slot] = own_hot(ids, count, "tall", 448, 60, 60, me.dp)
        pick(ordered, mid.at[slot], held[slot], out, flat, 16, 2, k)

    def pick_wide(k):
        if k == 0:
            turn(mid.at[0], turned, 0, 7)
            held[0] = own_hot(dids, dcount, "wide", 512, 60, 60, me.dp)
        order(turned, swap16, ordered, 16, 14, 1, k)
        pick(ordered, cot, held[0], od, flat, 16, 1, k)

    for k in range(4):
        work.append(lambda k=k: pick_tall(k, 1, og))
        work.append(lambda k=k: pick_tall(k, 2, ou))
    for k in range(4):
        work.append(lambda k=k: pick_wide(k))

    spread_ig = Spread(me, ig, sem_ig, 2)
    for h in range(2):
        cols = slice(h * 512, (h + 1) * 512)
        total = edge[1, :, cols] + backward.total(h)
        spread_ig.over_z(total.astype(BF), h)
        swap_from[0, :, cols] = total
    swap_ig = swap_out(me, swap_from.at[0], swap_to.at[0], sem_swap, 1)
    for copy in mid_far:
        copy.wait_recv()
    spot = mid.at[:, pl.ds(pl.multiple_of(((me.dp + 2) % 4) * 128, 128), 128), :]
    mid_cores.append(send(spot, spot, sem_mid, 11, me.sibling()))
    spread_cot.finish()
    for copy in mid_cores:
        copy.wait_recv()
    fill(1)
    spread_ig.over_x(None, 0)
    spread_ig.over_x(None, 1)
    spread_ig.widen()
    forward.over_z()
    fill(2)

    rows = spread_ig.group()
    near_sums[me.y] = dot_nt(ig[rows, :], wh[...]).astype(BF)
    spot = near_sums.at[me.y]
    cg_copies = [send(spot, spot, sem_cg, k - 1, me.at_y(k)) for k in range(1, me.tall)]
    spread_ig.forward()
    fill(3)
    spread_ig.over_cores()

    swap_from[1] = res[spread_res.chunk(me.z), home].astype(F32) + forward.total()
    swap_layer = swap_out(me, swap_from.at[1], swap_to.at[1], sem_swap, 2)
    ctx_copies[1].wait_recv()
    spot = ctx.at[pl.ds(pl.multiple_of(((me.dp + 2) % 4) * 128, 128), 128), :]
    ctx_copies.append(send(spot, spot, sem_ctx, 2, me.sibling()))
    fill(len(work))
    swap_ig.wait_recv()
    input_grad[...] = swap_to[0].astype(BF)

    for copy in cg_copies:
        copy.wait_recv()
    total = near_sums[0].astype(F32)
    for k in range(1, me.tall):
        total = total + near_sums[k].astype(F32)
    context_grad[...] = total.astype(BF)
    swap_layer.wait_recv()
    layer[...] = swap_to[1].astype(BF)

    for copy in [ctx_copies[0], ctx_copies[2]]:
        copy.wait_recv()
    turn(ctx, turned, 0, 2)
    swap = swap_matrix(32, 8)
    hot = own_hot(hids, hcount, "heads", 256, 17, 17, me.dp)
    for k in range(2):
        order(turned, swap, ordered.at[pl.ds(k * 256, 256), :], 8, 4, 1, k)
    spread_ig.finish()
    for k in range(2):
        pick(ordered.at[pl.ds(k * 256, 256), :], ig, hot, oh, flat, 8, 1, k)
    for part in (spread_cot, spread_res, spread_ig, attention, backward, forward):
        part.drain()
    late = [entry, swap_ig, swap_layer, mid_across]
    late += ctx_copies + mid_deltas + mid_hidden + mid_far + mid_cores + cg_copies
    for slot in range(3):
        late += sum_copies[slot]
    for copy in late:
        copy.wait_send()


def chain_call(x8, cot8, context, lists, gate, up, down, heads):
    def sds(*shape):
        return jax.ShapeDtypeStruct(shape, BF)

    shapes = [
        sds(8, 2048), sds(8, 2048), sds(128, 256),
        sds(60, CELL), sds(60, CELL), sds(60, CELL), sds(17, CELL),
    ]
    dma = pltpu.SemaphoreType.DMA
    tall = lax.axis_size("in")
    depth = lax.axis_size("out") // 2
    return pl.pallas_call(
        chain_kernel,
        out_shape=shapes,
        in_specs=[VM] * 11 + [ANY] * 3 + [VM],
        out_specs=[VM] * 7,
        scratch_shapes=[
            pltpu.VMEM((512, 2048), BF),
            pltpu.VMEM((512, 256), BF),
            pltpu.VMEM((512, 2048), BF),
            pltpu.VMEM((512, 2048), BF),
            pltpu.VMEM((3, 512, 896), BF),
            pltpu.VMEM((2048, 512), BF),
            pltpu.VMEM((512, 512), BF),
            pltpu.VMEM((512, 2048), BF),
            pltpu.VMEM((240, CELL), BF),
            pltpu.VMEM((240, CELL), BF),
            pltpu.VMEM((240, CELL), BF),
            pltpu.VMEM((512, 2048), BF),
            pltpu.VMEM((2048, 896), BF),
            pltpu.VMEM((2048, 896), BF),
            pltpu.VMEM((896, 2048), BF),
            pltpu.VMEM((256, 2048), BF),
            pltpu.VMEM((128, 2048), BF),
            pltpu.VMEM((2, 8, 2048), F32),
            pltpu.VMEM((2, 16, 1024), F32),
            pltpu.VMEM((3, 128, 1024), BF),
            pltpu.VMEM((3, 128, 1024), BF),
            pltpu.VMEM((3, depth - 1, 16, 1024), BF),
            pltpu.VMEM((2, 128, 2048), BF),
            pltpu.VMEM((3, 128, 896), F32),
            pltpu.VMEM((3, 128, 896), BF),
            pltpu.VMEM((tall - 1, 3, 32, 896), BF),
            pltpu.VMEM((2, 16, 1024), F32),
            pltpu.VMEM((2, 8, 2048), F32),
            pltpu.VMEM((tall, 128, 256), BF),
            dma((3,)),
            dma((2, 37)),
            dma((2, 37)),
            dma((2, 37)),
            dma((3, 2, 32)),
            dma((2, 3)),
            dma((3, 2, 3)),
            dma((2, 12)),
            dma((2, 3)),
            dma((2, 3)),
        ],
        compiler_params=pltpu.CompilerParams(
            collective_id=0, has_side_effects=True, vmem_limit_bytes=58 * 2**20
        ),
        name="chain",
    )(x8, cot8, context, *lists, gate, up, down, heads)


def local(
    inputs, context,
    gate_blocks, gate_ids, gate_count,
    up_blocks, up_ids, up_count,
    down_blocks, down_ids, down_count,
    heads_blocks, heads_ids, heads_count,
    cotangent,
):
    rows = lambda blocks: blocks.reshape(-1, CELL)
    line = lambda ids: ids.reshape(1, -1)
    lists = (
        line(gate_ids), gate_count, line(up_ids), up_count,
        line(down_ids), down_count, line(heads_ids), heads_count,
    )
    results = chain_call(
        inputs, cotangent, context, lists,
        rows(gate_blocks), rows(up_blocks), rows(down_blocks), rows(heads_blocks),
    )
    done = finish_call(*results)
    return (*done[:3], *(g.reshape(1, 1, -1, CELL) for g in done[3:]))


def solution(mesh):
    rows = P(("dp", "out"), "in")
    tall, wide = ("in", "out"), ("out", "in")

    def lists(axes):
        return P(*axes, None, None), P(*axes, None), P(*axes)

    return jax.shard_map(
        local,
        mesh=mesh,
        in_specs=(rows, P("dp", "out"), *lists(tall), *lists(tall), *lists(wide), *lists(wide), rows),
        out_specs=(
            rows,
            rows,
            P("dp", "out"),
            P(*tall, "dp", None),
            P(*tall, "dp", None),
            P(*wide, "dp", None),
            P(*wide, "dp", None),
        ),
        check_vma=False,
    )
```

```python
import jax
import jax.numpy as jnp
from jax import lax
from jax.experimental import pallas as pl
from jax.experimental.pallas import tpu as pltpu
from jax.sharding import PartitionSpec as P

BLOCK = 64
CELL = BLOCK * BLOCK
BF = jnp.bfloat16
F32 = jnp.float32
MESH = pl.DeviceIdType.MESH
VM = pl.BlockSpec(memory_space=pltpu.VMEM)
ANY = pl.BlockSpec(memory_space=pl.ANY)


def dot(a, b):
    return lax.dot_general(a, b, (((1,), (0,)), ((), ())), preferred_element_type=F32)


def dot_nt(a, b):
    return lax.dot_general(a, b, (((1,), (1,)), ((), ())), preferred_element_type=F32)


def dot_tn(a, b):
    return lax.dot_general(a, b, (((0,), (0,)), ((), ())), preferred_element_type=F32)


def one_hot(row, positions):
    spots = lax.broadcasted_iota(jnp.int32, (positions, row.shape[1]), 0)
    return jnp.where(spots == row, 1.0, 0.0).astype(BF)


def swap_matrix(inner, outer):
    rows = lax.broadcasted_iota(jnp.int32, (inner * outer, inner * outer), 0)
    cols = lax.broadcasted_iota(jnp.int32, (inner * outer, inner * outer), 1)
    source = (rows % outer) * inner + rows // outer
    return jnp.where(cols == source, 1.0, 0.0).astype(BF)


def halves(first, second):
    low = lax.broadcasted_iota(jnp.int32, first.shape, 1) < BLOCK
    return (
        jnp.where(low, first, pltpu.roll(second, BLOCK, 1)),
        jnp.where(low, pltpu.roll(first, BLOCK, 1), second),
    )


def spots(ids, count, kind):
    i = ids[...]
    if kind == "tall":
        r = (i * 2341) >> 15
        c = i - 14 * r
        spot = (r >> 4) * 224 + c * 16 + (r & 15)
    elif kind == "wide":
        spot = (i & 31) * 16 + (i >> 5)
    else:
        spot = (i & 31) * 8 + (i >> 5)
    slots = lax.broadcasted_iota(jnp.int32, i.shape, 1)
    return jnp.where(slots < count[...], spot, -1)


def place(hot, swap, blocks, stage, out, inner, used, stripes, k):
    chunk = 256 // inner
    width = out.shape[1]
    per = (width // BLOCK) * inner
    flat = dot(hot, blocks[:, k * chunk * BLOCK:(k + 1) * chunk * BLOCK]).astype(BF)
    for s in range(stripes):
        for p in range(chunk // 2):
            for q in range(width // 128):
                at = s * per + 2 * q * inner
                left = flat[at:at + inner, p * 128:(p + 1) * 128]
                right = flat[at + inner:at + 2 * inner, p * 128:(p + 1) * 128]
                pair = jnp.concatenate(halves(left, right), axis=0)
                at = s * 256 + 2 * p * inner
                stage[at:at + 2 * inner, q * 128:(q + 1) * 128] = pair
        dense = dot(swap, stage[s * 256:(s + 1) * 256, :width]).astype(BF)
        for r in range(used):
            at = s * inner * BLOCK + r * BLOCK + k * chunk
            out[at:at + chunk, :] = dense[r * chunk:(r + 1) * chunk]


def turn(left, turned, start, stop):
    for s in range(start, stop):
        turned[s * 128:(s + 1) * 128, :] = left[:, s * 128:(s + 1) * 128].T


def order(turned, swap, ordered, inner, used, stripes, k):
    chunk = 256 // inner
    for s in range(stripes):
        rows = [
            turned[s * used * BLOCK + r * BLOCK + k * chunk:s * used * BLOCK + r * BLOCK + (k + 1) * chunk, :]
            for r in range(used)
        ]
        rows += [jnp.zeros_like(rows[0])] * (inner - used)
        ordered[s * 256:(s + 1) * 256, :] = dot(swap, jnp.concatenate(rows, axis=0)).astype(BF)


def pick(ordered, right, hot, out, flat, inner, stripes, k):
    chunk = 256 // inner
    width = right.shape[1]
    piece = 1024 if width % 1024 == 0 else width
    for s in range(stripes):
        base = s * (width // BLOCK) * inner
        for t in range(width // piece):
            grad = dot(ordered[s * 256:(s + 1) * 256, :], right[:, t * piece:(t + 1) * piece]).astype(BF)
            for q in range(piece // 128):
                for p in range(chunk // 2):
                    pair = grad[2 * p * inner:(2 * p + 2) * inner, q * 128:(q + 1) * 128]
                    both = jnp.concatenate(halves(pair[:inner], pair[inner:]), axis=0)
                    at = base + (t * piece // 128 + q) * 2 * inner
                    flat[at:at + 2 * inner, p * 128:(p + 1) * 128] = both
    picked = dot_tn(hot, flat[:hot.shape[0], :chunk * BLOCK])
    out[:, k * chunk * BLOCK:(k + 1) * chunk * BLOCK] = picked.astype(BF)


def own_hot(ids, count, kind, positions, share, slots, dp):
    spot = spots(ids, count, kind)
    if slots > share:
        spot = jnp.concatenate([spot, jnp.full((1, slots - share), -1, jnp.int32)], axis=1)
    own = spot[:, :slots]
    for k in range(1, 4):
        own = jnp.where(dp == k, spot[:, k * share:k * share + slots], own)
    lanes = lax.broadcasted_iota(jnp.int32, own.shape, 1)
    return one_hot(jnp.where(lanes < share, own, -1), positions)


def finish_kernel(*refs):
    count = (len(refs) - 1) // 3
    sources, targets, held, sems = refs[:count], refs[count:2 * count], refs[2 * count:-1], refs[-1]
    loads = [pltpu.make_async_copy(sources[k], held[k], sems.at[0, k]) for k in range(count)]
    stores = [pltpu.make_async_copy(held[k], targets[k], sems.at[1, k]) for k in range(count)]
    for copy in loads:
        copy.start()
    for load, store in zip(loads, stores):
        load.wait()
        store.start()
    for copy in stores:
        copy.wait()


def finish_call(*results):
    return pl.pallas_call(
        finish_kernel,
        out_shape=[jax.ShapeDtypeStruct(r.shape, BF) for r in results],
        in_specs=[ANY] * len(results),
        out_specs=[ANY] * len(results),
        scratch_shapes=[pltpu.VMEM(r.shape, BF) for r in results]
        + [pltpu.SemaphoreType.DMA((2, len(results)))],
        compiler_params=pltpu.CompilerParams(vmem_limit_bytes=58 * 2**20),
        name="finish",
    )(*results)


class Links:

    def __init__(self):
        self.dp, self.y, self.out = lax.axis_index("dp"), lax.axis_index("in"), lax.axis_index("out")
        self.depth = lax.axis_size("out") // 2
        self.tall = lax.axis_size("in")
        self.core, self.z = self.dp % 2, self.out // 2
        self.low = self.out % 2
        self.x = (self.dp // 2) * 2 + self.low

    def at_x(self, k):
        x = (self.x + k) % 4
        return (x // 2) * 2 + self.core, self.y, self.z * 2 + x % 2

    def at_z(self, k):
        return self.dp, self.y, ((self.z + k) % self.depth) * 2 + self.low

    def at_y(self, k):
        return self.dp, (self.y + k) % self.tall, self.out

    def sibling(self):
        return (self.dp // 2) * 2 + 1 - self.core, self.y, self.out

    def beside(self):
        return self.dp, self.y, self.z * 2 + 1 - self.low

    def across(self):
        return (self.dp + 2) % 4, self.y, self.out

    def greet(self):
        barrier = pltpu.get_barrier_semaphore()
        peers = [self.at_x(k) for k in (1, 2, 3)]
        peers += [self.at_z(k) for k in range(1, self.depth)]
        peers += [self.at_y(k) for k in range(1, self.tall)]
        peers += [self.sibling()]
        for peer in peers:
            pl.semaphore_signal(barrier, inc=1, device_id=peer, device_id_type=MESH)
        return barrier, len(peers)

    def meet(self, greeted):
        pl.semaphore_wait(*greeted)


def send(source, target, sems, k, to):
    copy = pltpu.make_async_remote_copy(
        src_ref=source,
        dst_ref=target,
        send_sem=sems.at[0, k],
        recv_sem=sems.at[1, k],
        device_id=to,
        device_id_type=MESH,
    )
    copy.start()
    return copy


class Spread:

    def __init__(self, me, whole, sems, splits=1):
        self.me, self.whole, self.sems, self.width = me, whole, sems, 1024 // splits
        self.home = pl.ds(pl.multiple_of(me.low * 1024, 1024), 1024)
        self.away = pl.ds(pl.multiple_of((1 - me.low) * 1024, 1024), 1024)
        self.other = (me.dp + 2) % 4
        self.far = me.at_x(jnp.where(me.low == 0, 3, 1))
        self.sent, self.first, self.near = [], {}, []

    def rows(self, dp, start=0, size=128):
        return pl.ds(pl.multiple_of(dp * 128 + start, 16), size)

    def move(self, rows, lanes, k, to):
        spot = self.whole.at[rows, lanes]
        copy = send(spot, spot, self.sems, k, to)
        self.sent.append(copy)
        return copy

    def chunk(self, z):
        return pl.ds(pl.multiple_of(self.me.dp * 128 + (z % self.me.depth) * 16, 16), 16)

    def part(self, h):
        return pl.ds(pl.multiple_of(self.me.low * 1024 + h * self.width, self.width), self.width)

    def over_z(self, own, h=0):
        me = self.me
        self.whole[self.chunk(me.z), self.part(h)] = own
        ks = sorted(range(1, me.depth), key=lambda k: -min(k, me.depth - k))
        self.first[h] = {
            k: self.move(self.chunk(me.z), self.part(h), h * 8 + k, me.at_z(k)) for k in ks
        }

    def over_x(self, between=None, h=0):
        me, depth = self.me, self.me.depth
        at = 16 + h * 8
        self.near.append(self.move(self.chunk(me.z), self.part(h), at, me.beside()))
        for k in sorted(range(1, depth), key=lambda k: min(k, depth - k)):
            if between is not None and 2 < k < depth - k + 1:
                between(1)
            self.first[h][k].wait_recv()
            self.near.append(self.move(self.chunk(me.z + depth - k), self.part(h), at + k, me.beside()))

    def widen(self):
        self.wide = self.move(self.rows(self.me.dp), self.home, 32, self.far)

    def group(self):
        for copy in self.near:
            copy.wait_recv()
        return self.rows(self.me.dp)

    def forward(self):
        me = self.me
        self.half_a = self.move(self.rows(me.dp, 0, 64), self.away, 33, self.far)
        self.cores = [self.move(self.rows(me.dp), slice(None), 35, me.sibling())]
        self.wide.wait_recv()
        self.half_b = self.move(self.rows(self.other, 64, 64), self.away, 34, me.beside())

    def over_cores(self):
        self.half_a.wait_recv()
        self.half_b.wait_recv()
        self.cores.append(self.move(self.rows(self.other), slice(None), 36, self.me.sibling()))

    def finish(self):
        for copy in self.cores:
            copy.wait_recv()

    def drain(self):
        for copy in self.sent:
            copy.wait_send()


class Collect:

    def __init__(self, me, term, half, sums, parts, sems, splits=1):
        self.me, self.term, self.half, self.sums, self.parts, self.sems = me, term, half, sums, parts, sems
        self.width = 1024 // splits
        self.order = sorted(range(me.depth), key=lambda k: -min(k, me.depth - k))
        self.near, self.far, self.own = {}, {}, {}

    def chunk(self, k):
        return pl.ds(pl.multiple_of(((self.me.z + k) % self.me.depth) * 16, 16), 16)

    def lanes(self, h, low=0):
        return pl.ds(pl.multiple_of(low * 1024 + h * self.width, self.width), self.width)

    def over_x(self, h=0):
        for k in self.order:
            rows = self.chunk(k)
            self.near[h, k] = send(
                self.term.at[rows, self.lanes(h, 1 - self.me.low)], self.half.at[rows, self.lanes(h)],
                self.sems, h * 8 + k, self.me.beside(),
            )

    def over_z(self, h=0):
        me, lanes = self.me, self.lanes(h)
        for k in self.order:
            rows = self.chunk(k)
            self.near[h, k].wait_recv()
            both = self.term[rows, self.lanes(h, me.low)].astype(F32) + self.half[rows, lanes].astype(F32)
            if k == 0:
                self.own[h] = both
            else:
                self.sums[rows, lanes] = both.astype(BF)
                self.far[h, k] = send(
                    self.sums.at[rows, lanes], self.parts.at[k - 1, :, lanes], self.sems, 16 + h * 8 + k, me.at_z(k)
                )

    def total(self, h=0):
        total = self.own[h]
        for k in reversed(self.order[:-1]):
            self.far[h, k].wait_recv()
            total = total + self.parts[k - 1, :, self.lanes(h)].astype(F32)
        return total

    def drain(self):
        for copy in list(self.near.values()) + list(self.far.values()):
            copy.wait_send()


def swap_out(me, outgoing, landing, sems, k):
    away = outgoing.at[pl.ds(pl.multiple_of((1 - me.low) * 8, 8), 8), :]
    lanes = pl.ds(pl.multiple_of(me.low * 1024, 1024), 1024)
    landing[:, lanes] = outgoing[pl.ds(pl.multiple_of(me.low * 8, 8), 8), :]
    return send(away, landing.at[:, lanes], sems, k, me.beside())


def chain_kernel(
    x8, cot8, context, gids, gcount, uids, ucount, dids, dcount, hids, hcount, gate, up, down, heads,
    layer, input_grad, context_grad, og, ou, od, oh,
    ig, ctx, res, cot, mid, turned, ordered, flat, gate_in, up_in, down_in, stage, wg, wu, wd, wh, term,
    cells, edge, halves_in, sums, parts, backs,
    shares, shares_bf, gathered, swap_from, swap_to, near_sums,
    sem_in, sem_res, sem_cot, sem_ig, sem_rs, sem_ctx, sem_sum, sem_mid, sem_cg, sem_swap,
):
    loads = []
    for k, (source, target) in enumerate(((gate, gate_in), (up, up_in), (down, down_in))):
        loads.append(pltpu.make_async_copy(source, target, sem_in.at[k]))
        loads[-1].start()
    me = Links()
    greeted = me.greet()
    hot = one_hot(spots(hids, hcount, "heads"), 256)
    swap = swap_matrix(8, 32)
    for k in range(2):
        place(hot, swap, heads, stage, wh, 8, 4, 1, k)
    for t in range(2):
        cols = slice(t * 1024, (t + 1) * 1024)
        term[:, cols] = dot(context[...], wh[:, cols]).astype(BF)

    swap16 = swap_matrix(16, 16)
    work = []

    def queue(load, ids, count, kind, blocks, out, stripes, used):
        held = {}

        def step(k):
            if k == 0:
                loads[load].wait()
                held["hot"] = one_hot(spots(ids, count, kind), 448 if kind == "tall" else 512)
            place(held["hot"], swap16, blocks, stage, out, 16, used, stripes, k)

        for k in range(4):
            work.append(lambda k=k: step(k))

    queue(0, gids, gcount, "tall", gate_in, wg, 2, 16)
    queue(1, uids, ucount, "tall", up_in, wu, 2, 16)
    queue(2, dids, dcount, "wide", down_in, wd, 1, 14)

    def fill(n):
        for _ in range(n):
            work.pop(0)()

    low8 = pl.ds(pl.multiple_of(me.low * 8, 8), 8)
    away = pl.ds(pl.multiple_of((1 - me.low) * 1024, 1024), 1024)
    home = pl.ds(pl.multiple_of(me.low * 1024, 1024), 1024)

    def collect(term, k):
        return Collect(me, term, halves_in.at[k], sums.at[k], parts.at[k], sem_rs.at[k], 1 if k == 2 else 2)

    cells[0] = x8[...].astype(F32)
    cells[1] = cot8[...].astype(F32)
    edge[:, low8, :] = cells[:, :, home]
    me.meet(greeted)
    attention = collect(term, 0)
    attention.over_x(0)
    entry = send(cells.at[:, :, away], edge.at[:, low8, :], sem_swap, 0, me.beside())
    attention.over_x(1)
    fill(2)
    attention.over_z(0)
    fill(1)
    attention.over_z(1)
    entry.wait_recv()
    spread_cot = Spread(me, cot, sem_cot)
    spread_cot.over_z(edge[1].astype(BF))
    own_ctx = pl.ds(pl.multiple_of(me.dp * 128, 128), 128)
    ctx[own_ctx, :] = context[...]
    spot = ctx.at[own_ctx, :]
    ctx_copies = [send(spot, spot, sem_ctx, k, to) for k, to in enumerate((me.sibling(), me.across()))]
    fill(2)
    spread_res = Spread(me, res, sem_res, 2)
    for h in range(2):
        cols = slice(h * 512, (h + 1) * 512)
        spread_res.over_z((edge[0, :, cols] + attention.total(h)).astype(BF), h)
        fill(1)
    spread_cot.over_x()
    spread_cot.widen()
    fill(1)
    spread_res.over_x(None, 0)
    fill(1)
    spread_res.over_x(None, 1)
    spread_res.widen()
    fill(3)

    def share(slot):
        copies = []
        for k in range(1, me.tall):
            rows = pl.ds(pl.multiple_of(((me.y + k) % me.tall) * 32, 32), 32)
            copies.append(
                send(shares_bf.at[slot, rows, :], gathered.at[k - 1, slot], sem_sum.at[slot], k - 1, me.at_y(k))
            )
        return copies

    rows = spread_cot.group()
    for t in range(2):
        lanes = slice(t * 512, min(896, (t + 1) * 512))
        shares[2, :, lanes] = dot_nt(cot[rows, :], wd[lanes, :])
    shares_bf[2] = shares[2].astype(BF)
    sum_copies = {2: share(2)}

    rows = spread_res.group()
    for slot, weight in ((0, wg), (1, wu)):
        shares[slot] = dot(res[rows, :], weight[...])
        shares_bf[slot] = shares[slot].astype(BF)
        sum_copies[slot] = share(slot)

    spread_cot.forward()
    spread_res.forward()
    quarter = pl.ds(pl.multiple_of(me.y * 32, 32), 32)

    def total_of(slot):
        total = shares[slot, quarter, :]
        for k in range(me.tall - 1):
            sum_copies[slot][k].wait_recv()
            total = total + gathered[k, slot].astype(F32)
        return total

    hidden_grad = total_of(2)
    gate_sum = total_of(0)
    sigmoid = 1.0 / (1.0 + jnp.exp(-gate_sum))
    slope = hidden_grad * sigmoid * (1.0 + gate_sum * (1.0 - sigmoid))
    swish = gate_sum * sigmoid
    up_sum = total_of(1)
    spot_rows = pl.ds(pl.multiple_of(me.dp * 128 + me.y * 32, 32), 32)
    mid[1, spot_rows, :] = (slope * up_sum).astype(BF)
    mid[2, spot_rows, :] = (hidden_grad * swish).astype(BF)
    spot = mid.at[pl.ds(1, 2), spot_rows, :]
    mid_deltas = [send(spot, spot, sem_mid, k - 1, me.at_y(k)) for k in range(1, me.tall)]
    mid[0, spot_rows, :] = (swish * up_sum).astype(BF)
    spot = mid.at[0, spot_rows, :]
    mid_hidden = [send(spot, spot, sem_mid, 2 + k, me.at_y(k)) for k in range(1, me.tall)]
    spot = mid.at[:, spot_rows, :]
    mid_across = send(spot, spot, sem_mid, 6, me.across())
    spread_res.over_cores()
    spread_cot.over_cores()
    spread_res.finish()
    turn(res, turned, 0, 16)
    for copy in mid_deltas:
        copy.wait_recv()

    mid_across.wait_recv()
    spot = mid.at[:, pl.ds(pl.multiple_of(((me.dp + 2) % 4) * 128 + me.y * 32, 32), 32), :]
    mid_far = [send(spot, spot, sem_mid, 6 + k, me.at_y(k)) for k in range(1, me.tall)]

    rows = pl.ds(pl.multiple_of(me.dp * 128, 128), 128)
    backward = collect(backs.at[0], 1)
    for low in (1 - me.low, me.low):
        for h in range(2):
            lanes = pl.ds(pl.multiple_of(low * 1024 + h * 512, 512), 512)
            backs[0, :, lanes] = (
                dot_nt(mid[1, rows, :], wg[lanes, :]) + dot_nt(mid[2, rows, :], wu[lanes, :])
            ).astype(BF)
            if low is not me.low:
                backward.over_x(h)
    backward.over_z(0)
    backward.over_z(1)
    for copy in mid_hidden:
        copy.wait_recv()
    spot = mid.at[:, rows, :]
    mid_cores = [send(spot, spot, sem_mid, 10, me.sibling())]
    for t in range(2):
        lanes = slice(t * 1024, (t + 1) * 1024)
        backs[1, :, lanes] = dot(mid[0, rows, :], wd[:, lanes]).astype(BF)
    forward = collect(backs.at[1], 2)
    forward.over_x()

    held = {}

    def pick_tall(k, slot, out):
        if slot == 1:
            order(turned, swap16, ordered, 16, 16, 2, k)
        if slot not in held:
            ids, count = ((gids, gcount), (uids, ucount))[slot - 1]
            held[slot] = own_hot(ids, count, "tall", 448, 60, 60, me.dp)
        pick(ordered, mid.at[slot], held[slot], out, flat, 16, 2, k)

    def pick_wide(k):
        if k == 0:
            turn(mid.at[0], turned, 0, 7)
            held[0] = own_hot(dids, dcount, "wide", 512, 60, 60, me.dp)
        order(turned, swap16, ordered, 16, 14, 1, k)
        pick(ordered, cot, held[0], od, flat, 16, 1, k)

    for k in range(4):
        work.append(lambda k=k: pick_tall(k, 1, og))
        work.append(lambda k=k: pick_tall(k, 2, ou))
    for k in range(4):
        work.append(lambda k=k: pick_wide(k))

    spread_ig = Spread(me, ig, sem_ig, 2)
    for h in range(2):
        cols = slice(h * 512, (h + 1) * 512)
        total = edge[1, :, cols] + backward.total(h)
        spread_ig.over_z(total.astype(BF), h)
        swap_from[0, :, cols] = total
    swap_ig = swap_out(me, swap_from.at[0], swap_to.at[0], sem_swap, 1)
    for copy in mid_far:
        copy.wait_recv()
    spot = mid.at[:, pl.ds(pl.multiple_of(((me.dp + 2) % 4) * 128, 128), 128), :]
    mid_cores.append(send(spot, spot, sem_mid, 11, me.sibling()))
    spread_cot.finish()
    for copy in mid_cores:
        copy.wait_recv()
    fill(1)
    spread_ig.over_x(fill, 0)
    spread_ig.over_x(None, 1)
    spread_ig.widen()
    forward.over_z()
    fill(2)

    rows = spread_ig.group()
    spread_ig.forward()
    near_sums[me.y] = dot_nt(ig[rows, :], wh[...]).astype(BF)
    spot = near_sums.at[me.y]
    cg_copies = [send(spot, spot, sem_cg, k - 1, me.at_y(k)) for k in range(1, me.tall)]
    fill(3)
    spread_ig.over_cores()

    swap_from[1] = res[spread_res.chunk(me.z), home].astype(F32) + forward.total()
    swap_layer = swap_out(me, swap_from.at[1], swap_to.at[1], sem_swap, 2)
    ctx_copies[1].wait_recv()
    spot = ctx.at[pl.ds(pl.multiple_of(((me.dp + 2) % 4) * 128, 128), 128), :]
    ctx_copies.append(send(spot, spot, sem_ctx, 2, me.sibling()))
    fill(len(work))
    swap_ig.wait_recv()
    input_grad[...] = swap_to[0].astype(BF)

    for copy in cg_copies:
        copy.wait_recv()
    total = near_sums[0].astype(F32)
    for k in range(1, me.tall):
        total = total + near_sums[k].astype(F32)
    context_grad[...] = total.astype(BF)
    swap_layer.wait_recv()
    layer[...] = swap_to[1].astype(BF)

    for copy in [ctx_copies[0], ctx_copies[2]]:
        copy.wait_recv()
    turn(ctx, turned, 0, 2)
    swap = swap_matrix(32, 8)
    hot = own_hot(hids, hcount, "heads", 256, 17, 17, me.dp)
    for k in range(2):
        order(turned, swap, ordered.at[pl.ds(k * 256, 256), :], 8, 4, 1, k)
    spread_ig.finish()
    for k in range(2):
        pick(ordered.at[pl.ds(k * 256, 256), :], ig, hot, oh, flat, 8, 1, k)
    for part in (spread_cot, spread_res, spread_ig, attention, backward, forward):
        part.drain()
    late = [entry, swap_ig, swap_layer, mid_across]
    late += ctx_copies + mid_deltas + mid_hidden + mid_far + mid_cores + cg_copies
    for slot in range(3):
        late += sum_copies[slot]
    for copy in late:
        copy.wait_send()


def chain_call(x8, cot8, context, lists, gate, up, down, heads):
    def sds(*shape):
        return jax.ShapeDtypeStruct(shape, BF)

    shapes = [
        sds(8, 2048), sds(8, 2048), sds(128, 256),
        sds(60, CELL), sds(60, CELL), sds(60, CELL), sds(17, CELL),
    ]
    dma = pltpu.SemaphoreType.DMA
    tall = lax.axis_size("in")
    depth = lax.axis_size("out") // 2
    return pl.pallas_call(
        chain_kernel,
        out_shape=shapes,
        in_specs=[VM] * 11 + [ANY] * 3 + [VM],
        out_specs=[VM] * 7,
        scratch_shapes=[
            pltpu.VMEM((512, 2048), BF),
            pltpu.VMEM((512, 256), BF),
            pltpu.VMEM((512, 2048), BF),
            pltpu.VMEM((512, 2048), BF),
            pltpu.VMEM((3, 512, 896), BF),
            pltpu.VMEM((2048, 512), BF),
            pltpu.VMEM((512, 512), BF),
            pltpu.VMEM((512, 2048), BF),
            pltpu.VMEM((240, CELL), BF),
            pltpu.VMEM((240, CELL), BF),
            pltpu.VMEM((240, CELL), BF),
            pltpu.VMEM((512, 2048), BF),
            pltpu.VMEM((2048, 896), BF),
            pltpu.VMEM((2048, 896), BF),
            pltpu.VMEM((896, 2048), BF),
            pltpu.VMEM((256, 2048), BF),
            pltpu.VMEM((128, 2048), BF),
            pltpu.VMEM((2, 8, 2048), F32),
            pltpu.VMEM((2, 16, 1024), F32),
            pltpu.VMEM((3, 128, 1024), BF),
            pltpu.VMEM((3, 128, 1024), BF),
            pltpu.VMEM((3, depth - 1, 16, 1024), BF),
            pltpu.VMEM((2, 128, 2048), BF),
            pltpu.VMEM((3, 128, 896), F32),
            pltpu.VMEM((3, 128, 896), BF),
            pltpu.VMEM((tall - 1, 3, 32, 896), BF),
            pltpu.VMEM((2, 16, 1024), F32),
            pltpu.VMEM((2, 8, 2048), F32),
            pltpu.VMEM((tall, 128, 256), BF),
            dma((3,)),
            dma((2, 37)),
            dma((2, 37)),
            dma((2, 37)),
            dma((3, 2, 32)),
            dma((2, 3)),
            dma((3, 2, 3)),
            dma((2, 12)),
            dma((2, 3)),
            dma((2, 3)),
        ],
        compiler_params=pltpu.CompilerParams(
            collective_id=0, has_side_effects=True, vmem_limit_bytes=58 * 2**20
        ),
        name="chain",
    )(x8, cot8, context, *lists, gate, up, down, heads)


def local(
    inputs, context,
    gate_blocks, gate_ids, gate_count,
    up_blocks, up_ids, up_count,
    down_blocks, down_ids, down_count,
    heads_blocks, heads_ids, heads_count,
    cotangent,
):
    rows = lambda blocks: blocks.reshape(-1, CELL)
    line = lambda ids: ids.reshape(1, -1)
    lists = (
        line(gate_ids), gate_count, line(up_ids), up_count,
        line(down_ids), down_count, line(heads_ids), heads_count,
    )
    results = chain_call(
        inputs, cotangent, context, lists,
        rows(gate_blocks), rows(up_blocks), rows(down_blocks), rows(heads_blocks),
    )
    done = finish_call(*results)
    return (*done[:3], *(g.reshape(1, 1, -1, CELL) for g in done[3:]))


def solution(mesh):
    rows = P(("dp", "out"), "in")
    tall, wide = ("in", "out"), ("out", "in")

    def lists(axes):
        return P(*axes, None, None), P(*axes, None), P(*axes)

    return jax.shard_map(
        local,
        mesh=mesh,
        in_specs=(rows, P("dp", "out"), *lists(tall), *lists(tall), *lists(wide), *lists(wide), rows),
        out_specs=(
            rows,
            rows,
            P("dp", "out"),
            P(*tall, "dp", None),
            P(*tall, "dp", None),
            P(*wide, "dp", None),
            P(*wide, "dp", None),
        ),
        check_vma=False,
    )
```
